32 devices in a mesh: xd: 4 (over z), ta: 8 (over y, x, core).
Axes of the slice: x: 2, y: 2, z: 4, core: 2. Of those that a mesh axis runs over, the one named last changes fastest.
Arguments:
- gauge_links: float32 [4, 2, 3, 3, 16, 8, 4, 128], P(None, None, None, None, 'xd', 'ta'), may hold values from -1 to 1, as said below
- momenta: float32 [4, 2, 3, 3, 16, 8, 4, 128], P(None, None, None, None, 'xd', 'ta'), as said below
- noise_table: float32 [2, 4, 3, 4096], replicated, may hold values from -6 to 6
- noise_index: int32 [16, 8, 4, 128], P('xd', 'ta'), may hold values from 0 to 4095
- partner: int32 [16], P('xd'), may hold values from 0 to 15, as said below
Outputs:
- new_links: float32 [4, 2, 3, 3, 16, 8, 4, 128], P(None, None, None, None, 'xd', 'ta')
- new_momenta: float32 [4, 2, 3, 3, 16, 8, 4, 128], P(None, None, None, None, 'xd', 'ta')
The draws below stay inside these ranges and needn't reach their ends.
Inputs may be any that keep to these rules, and one draw needn't show every extreme that they name: partner is an involution without fixed points: each row x1 is paired with a row of the aligned block of 4 rows that lies 16 / 2 rows away, and partner[partner[x1]] = x1. Every gauge_links[mu] at every site is a special unitary 3 x 3 matrix. Every momenta[mu] at every site is a Hermitian traceless 3 x 3 matrix.
All inputs are finite; a program needn't handle non-finite values.
Results may differ from the reference program's by a relative error of at most 0.0001.
Values sent between devices are 32-bit elements; how exact they have to be, the bound alone decides.
A program may use at most 128 MiB of HBM per device.

```python
import jax
import jax.numpy as jnp

X1L = 4
N2 = 4
N3 = 128
MD_STEPS = 2
DEGREE = 6
NOISE = 4096
NX1 = 16
NT = 8


def complex_times(left_real, left_imag, right_real, right_imag):
    return (left_real * right_real - left_imag * right_imag, left_real * right_imag + left_imag * right_real)


def draw_gauge_links(key, part):
    key_real, key_imag = jax.random.split(key, 2)
    full_shape = (4, 3, 3, NX1, NT, N2, N3)
    base_real = jax.random.normal(key_real, full_shape, jnp.float32)
    base_imag = jax.random.normal(key_imag, full_shape, jnp.float32)
    first_real = base_real[:, 0]
    first_imag = base_imag[:, 0]
    length_first = jnp.sqrt(jnp.sum(first_real * first_real + first_imag * first_imag, axis=1, keepdims=True)) + 1e-06
    first_real = first_real / length_first
    first_imag = first_imag / length_first
    second_real = base_real[:, 1]
    second_imag = base_imag[:, 1]
    inner_real = jnp.sum(first_real * second_real + first_imag * second_imag, axis=1, keepdims=True)
    inner_imag = jnp.sum(first_real * second_imag - first_imag * second_real, axis=1, keepdims=True)
    proj_real, proj_imag = complex_times(inner_real, inner_imag, first_real, first_imag)
    second_real = second_real - proj_real
    second_imag = second_imag - proj_imag
    length_second = jnp.sqrt(jnp.sum(second_real * second_real + second_imag * second_imag, axis=1, keepdims=True)) + 1e-06
    second_real = second_real / length_second
    second_imag = second_imag / length_second
    third_real = []
    third_imag = []
    for colour in range(3):
        next_one = (colour + 1) % 3
        next_two = (colour + 2) % 3
        prod_real, prod_imag = complex_times(first_real[:, next_one], first_imag[:, next_one], second_real[:, next_two], second_imag[:, next_two])
        back_real, back_imag = complex_times(first_real[:, next_two], first_imag[:, next_two], second_real[:, next_one], second_imag[:, next_one])
        third_real.append(prod_real - back_real)
        third_imag.append(-(prod_imag - back_imag))
    whole_real = jnp.stack([first_real, second_real, jnp.stack(third_real, axis=1)], axis=1)
    whole_imag = jnp.stack([first_imag, second_imag, jnp.stack(third_imag, axis=1)], axis=1)
    return jnp.stack([whole_real, whole_imag], axis=1)


def draw_momenta(key, part):
    key_real, key_imag = jax.random.split(jax.random.fold_in(key, 7), 2)
    full_shape = (4, 3, 3, NX1, NT, N2, N3)
    base_real = jax.random.normal(key_real, full_shape, jnp.float32)
    base_imag = jax.random.normal(key_imag, full_shape, jnp.float32)
    herm_real = (base_real + jnp.swapaxes(base_real, 1, 2)) * 0.5
    herm_imag = (base_imag - jnp.swapaxes(base_imag, 1, 2)) * 0.5
    trace_third = (herm_real[:, 0, 0] + herm_real[:, 1, 1] + herm_real[:, 2, 2]) / 3.0
    identity = jnp.eye(3, dtype=jnp.float32)[None, :, :, None, None, None, None]
    herm_real = herm_real - identity * trace_third[:, None, None]
    return jnp.stack([herm_real, herm_imag], axis=1)


def one_shuffle(one_key):
    return jax.random.permutation(one_key, X1L)


def draw_partner(key, part):
    block_count = NX1 // X1L
    half_count = block_count // 2
    keys_list = jax.random.split(jax.random.fold_in(key, 11), half_count)
    shuffles = jax.vmap(one_shuffle)(keys_list).astype(jnp.int32)
    inverse = jnp.argsort(shuffles, axis=1, stable=True).astype(jnp.int32)
    block_start = jnp.arange(half_count, dtype=jnp.int32)[:, None] * X1L
    lower_half = block_start + half_count * X1L + shuffles
    upper_half = block_start + inverse
    return jnp.concatenate([lower_half.reshape(-1), upper_half.reshape(-1)]).astype(jnp.int32)


def with_ends(drawn, rng, smallest, largest):
    dims = drawn.shape
    index_at = [jax.random.randint(jax.random.fold_in(rng, axis), (), 0, dims[axis]) for axis in range(len(dims))]
    drawn = drawn.at[tuple(index_at)].set(smallest)
    longest = dims.index(max(dims))
    index_at[longest] = (index_at[longest] + 1) % dims[longest]
    return drawn.at[tuple(index_at)].set(largest)


def noise(key, extent, spread, bound, kind=jnp.bfloat16):
    values = jax.random.normal(key, extent, jnp.float32) * spread
    return jnp.minimum(jnp.maximum(values, -bound), bound).astype(kind)


def setup_inputs(seed: int = 0) -> dict:
    streams_of = jax.random.split(jax.random.key(seed), 6)
    gauge_links = draw_gauge_links(jax.random.fold_in(streams_of[5], 71), 0)
    momenta = draw_momenta(jax.random.fold_in(streams_of[5], 71), 0)
    noise_table = noise(streams_of[2], (2, 4, 3, NOISE), 1.0, 6.0, jnp.float32)
    noise_index = with_ends(jax.random.randint(streams_of[3], (NX1, NT, N2, N3), 0, NOISE), jax.random.fold_in(streams_of[3], 1), 0, NOISE - 1).astype(jnp.int32)
    partner = draw_partner(jax.random.fold_in(streams_of[5], 71), 0)
    return {"gauge_links": gauge_links, "momenta": momenta, "noise_table": noise_table, "noise_index": noise_index, "partner": partner}


hopping = 0.13
step_size = 0.25

gamma_table = (
    ((3, 2, 1, 0), (0, 0, 0, 0), (1, 1, -1, -1)),
    ((2, 3, 0, 1), (1, 1, 1, 1), (0, 0, 0, 0)),
    ((3, 2, 1, 0), (-1, 1, 1, -1), (0, 0, 0, 0)),
    ((2, 3, 0, 1), (0, 0, 0, 0), (1, -1, -1, 1)),
)


def spin_apply(spinor, direction, sign_factor):
    source_order, real_part, imag_part = gamma_table[direction]
    rows_real = []
    rows_imag = []
    for spin_row in range(4):
        source = source_order[spin_row]
        add_real = spinor[0, source] * (sign_factor * real_part[spin_row]) - spinor[1, source] * (sign_factor * imag_part[spin_row])
        add_imag = spinor[1, source] * (sign_factor * real_part[spin_row]) + spinor[0, source] * (sign_factor * imag_part[spin_row])
        rows_real.append(spinor[0, spin_row] + add_real)
        rows_imag.append(spinor[1, spin_row] + add_imag)
    return jnp.stack([jnp.stack(rows_real), jnp.stack(rows_imag)])


def mat_vec(matrix, spinor):
    mat_real = matrix[0][None]
    mat_imag = matrix[1][None]
    vec_real = spinor[0][:, None]
    vec_imag = spinor[1][:, None]
    out_real = jnp.sum(mat_real * vec_real - mat_imag * vec_imag, axis=2)
    out_imag = jnp.sum(mat_real * vec_imag + mat_imag * vec_real, axis=2)
    return jnp.stack([out_real, out_imag])


def dagger(matrix):
    return jnp.stack([jnp.swapaxes(matrix[0], 0, 1), -jnp.swapaxes(matrix[1], 0, 1)])


def mat_mat(left_mat, right_mat):
    left_real = left_mat[0][:, :, None]
    left_imag = left_mat[1][:, :, None]
    right_real = right_mat[0][None]
    right_imag = right_mat[1][None]
    return jnp.stack([jnp.sum(left_real * right_real - left_imag * right_imag, axis=1),
                      jnp.sum(left_real * right_imag + left_imag * right_real, axis=1)])


def outer_sum(first_spin, second_spin):
    first_real = first_spin[0][:, :, None]
    first_imag = first_spin[1][:, :, None]
    second_real = second_spin[0][:, None]
    second_imag = second_spin[1][:, None]
    return jnp.stack([jnp.sum(first_real * second_real + first_imag * second_imag, axis=0),
                      jnp.sum(first_imag * second_real - first_real * second_imag, axis=0)])


def hermitian_part(matrix):
    swap_real = jnp.swapaxes(matrix[0], 0, 1)
    swap_imag = jnp.swapaxes(matrix[1], 0, 1)
    part_real = (matrix[1] + swap_imag) * 0.5
    part_imag = (swap_real - matrix[0]) * 0.5
    trace_third = (matrix[1][0, 0] + matrix[1][1, 1] + matrix[1][2, 2]) / 3.0
    identity = jnp.eye(3, dtype=jnp.float32).reshape((3, 3) + (1,) * (matrix.ndim - 3))
    return jnp.stack([part_real - identity * trace_third, part_imag])


def step_up(spinor, direction, partner):
    if direction == 0:
        return jnp.roll(spinor, -1, axis=-4)
    if direction == 1:
        time_index = jnp.arange(spinor.shape[-3])
        flip_sign = jnp.where(time_index == spinor.shape[-3] - 1, -1.0, 1.0).astype(jnp.float32)
        return jnp.roll(spinor, -1, axis=-3) * flip_sign[:, None, None]
    if direction == 2:
        wrapped = jnp.take(spinor[..., :1, :], partner, axis=-4)
        return jnp.concatenate([spinor[..., 1:, :], wrapped], axis=-2)
    return jnp.roll(spinor, -1, axis=-1)


def step_down(spinor, direction, partner):
    if direction == 0:
        return jnp.roll(spinor, 1, axis=-4)
    if direction == 1:
        time_index = jnp.arange(spinor.shape[-3])
        flip_sign = jnp.where(time_index == 0, -1.0, 1.0).astype(jnp.float32)
        return jnp.roll(spinor, 1, axis=-3) * flip_sign[:, None, None]
    if direction == 2:
        wrapped = jnp.take(spinor[..., -1:, :], partner, axis=-4)
        return jnp.concatenate([wrapped, spinor[..., :-1, :]], axis=-2)
    return jnp.roll(spinor, 1, axis=-1)


def dirac_dag(gauge_links, spinor, partner):
    hop_sum = None
    for direction in range(4):
        ahead = mat_vec(gauge_links[direction], step_up(spinor, direction, partner))
        behind = step_down(mat_vec(dagger(gauge_links[direction]), spinor), direction, partner)
        hop_term = spin_apply(ahead, direction, 1) + spin_apply(behind, direction, -1)
        hop_sum = hop_term if direction == 0 else hop_sum + hop_term
    return spinor - hopping * hop_sum


def force_term(gauge_links, phi, response, partner):
    forces = []
    for direction in range(4):
        ahead_field = spin_apply(step_up(response, direction, partner), direction, -1)
        local_field = spin_apply(response, direction, 1)
        bracket = outer_sum(ahead_field, phi) + outer_sum(step_up(phi, direction, partner), local_field)
        forces.append(hermitian_part(mat_mat(gauge_links[direction], bracket)) * (-2.0 * hopping))
    return jnp.stack(forces)


def link_update(momenta, gauge_links):
    identity = jnp.stack([jnp.eye(3, dtype=jnp.float32), jnp.zeros((3, 3), jnp.float32)]).reshape(2, 3, 3, 1, 1, 1, 1)
    updated = []
    for direction in range(4):
        generator = jnp.stack([-step_size * momenta[direction, 1], step_size * momenta[direction, 0]])
        series = identity
        for term_index in range(DEGREE, 0, -1):
            series = identity + mat_mat(generator, series) / float(term_index)
        updated.append(mat_mat(series, gauge_links[direction]))
    return jnp.stack(updated)


def reference(gauge_links, momenta, noise_table, noise_index, partner):
    noise_field = jnp.take(noise_table, noise_index, axis=3)
    phi = dirac_dag(gauge_links, noise_field, partner)
    for step_number in range(MD_STEPS):
        response = dirac_dag(gauge_links, phi, partner)
        forces = force_term(gauge_links, phi, response, partner)
        mirrored = jnp.take(forces, partner, axis=-4)
        total_force = jnp.stack([forces[:, 0] - mirrored[:, 0], forces[:, 1] + mirrored[:, 1]], axis=1)
        momenta = momenta + step_size * total_force
        gauge_links = link_update(momenta, gauge_links)
    return gauge_links, momenta
```

```python
import functools

import jax
import jax.numpy as jnp
from jax import lax
from jax.experimental import pallas as pl
from jax.experimental.pallas import tpu as pltpu
from jax.sharding import PartitionSpec as P

MESH = pl.DeviceIdType.MESH
F32 = jnp.float32

MD_STEPS = 2

hopping = 0.13
step_size = 0.25
gamma_table = (
    ((3, 2, 1, 0), (0, 0, 0, 0), (1, 1, -1, -1)),
    ((2, 3, 0, 1), (1, 1, 1, 1), (0, 0, 0, 0)),
    ((3, 2, 1, 0), (-1, 1, 1, -1), (0, 0, 0, 0)),
    ((2, 3, 0, 1), (0, 0, 0, 0), (1, -1, -1, 1)),
)


def noise_kernel(table, index, out):
    rows, lanes = index.shape
    entries = table.shape[-1]
    lane = jnp.bitwise_and(index[...], lanes - 1)
    chunk = lax.div(index[...], lanes)

    def one(k, carry):
        for colour in range(3):
            total = jnp.zeros((rows, lanes), F32)
            for c in range(entries // lanes):
                row = table[k, colour : colour + 1, c * lanes : (c + 1) * lanes]
                value = jnp.take_along_axis(
                    jnp.broadcast_to(row, (rows, lanes)), lane, axis=1, mode="promise_in_bounds"
                )
                total = jnp.where(chunk == c, value, total)
            out[k, colour] = total
        return carry

    lax.fori_loop(0, 8, one, 0)


def times_i(re, im, g_re, g_im):
    if g_re == 1:
        return re, im
    if g_re == -1:
        return -re, -im
    if g_im == 1:
        return -im, re
    return im, -re


def project(spinor, mu, sign):
    order, g_re, g_im = gamma_table[mu]
    out_re, out_im = [], []
    for s in range(2):
        add_re, add_im = times_i(
            spinor[0, order[s]], spinor[1, order[s]], sign * g_re[s], sign * g_im[s]
        )
        out_re.append(spinor[0, s] + add_re)
        out_im.append(spinor[1, s] + add_im)
    return jnp.stack(out_re), jnp.stack(out_im)


def mat_vec(links, mu, half):
    re, im = half
    out_re = out_im = None
    for b in range(3):
        m_re, m_im = links[mu, 0, :, b][None], links[mu, 1, :, b][None]
        v_re, v_im = re[:, b : b + 1], im[:, b : b + 1]
        t_re = m_re * v_re - m_im * v_im
        t_im = m_re * v_im + m_im * v_re
        out_re = t_re if b == 0 else out_re + t_re
        out_im = t_im if b == 0 else out_im + t_im
    return out_re, out_im


def dag_vec(links, mu, half):
    re, im = half
    out_re = out_im = None
    for b in range(3):
        m_re, m_im = links[mu, 0, b][None], links[mu, 1, b][None]
        v_re, v_im = re[:, b : b + 1], im[:, b : b + 1]
        t_re = m_re * v_re + m_im * v_im
        t_im = m_re * v_im - m_im * v_re
        out_re = t_re if b == 0 else out_re + t_re
        out_im = t_im if b == 0 else out_im + t_im
    return out_re, out_im


def outer(first, second):
    out_re = out_im = None
    for s in range(2):
        f_re, f_im = first[0][s][:, None], first[1][s][:, None]
        g_re, g_im = second[0][s][None], second[1][s][None]
        t_re = f_re * g_re + f_im * g_im
        t_im = f_im * g_re - f_re * g_im
        out_re = t_re if s == 0 else out_re + t_re
        out_im = t_im if s == 0 else out_im + t_im
    return out_re, out_im


def complex_times(a, b):
    return a[0] * b[0] - a[1] * b[1], a[0] * b[1] + a[1] * b[0]


def complex_by_conj(a, b):
    return a[0] * b[0] + a[1] * b[1], a[1] * b[0] - a[0] * b[1]


def square(c):
    return c[0] * c[0] + c[1] * c[1]


def link_exponential(p):
    b = [step_size * part for part in p]
    d0, d1 = b[0], b[1]
    d2 = -(d0 + d1)
    o01, o02, o12 = (b[2], b[3]), (b[4], b[5]), (b[6], b[7])
    n01, n02, n12 = square(o01), square(o02), square(o12)
    s0 = d0 * d0 + n01 + n02
    s1 = d1 * d1 + n01 + n12
    s2 = d2 * d2 + n02 + n12
    r01 = complex_by_conj(o02, o12)
    r02 = complex_times(o01, o12)
    r12 = complex_times((o01[0], -o01[1]), o02)
    s01 = (r01[0] - d2 * o01[0], r01[1] - d2 * o01[1])
    s02 = (r02[0] - d1 * o02[0], r02[1] - d1 * o02[1])
    s12 = (r12[0] - d0 * o12[0], r12[1] - d0 * o12[1])
    c1 = 0.5 * (s0 + s1 + s2)
    c0 = (
        d0 * (d1 * d2 - n12) - d1 * n02 - d2 * n01
        + 2.0 * (r02[0] * o02[0] + r02[1] * o02[1])
    )
    q0 = (1.0 - c0 * c0 * (1.0 / 720.0), c0 * (c1 * (1.0 / 120.0) - 1.0 / 6.0))
    q1 = (c0 * (1.0 / 24.0 - c1 * (1.0 / 360.0)), 1.0 + c1 * (c1 * (1.0 / 120.0) - 1.0 / 6.0))
    q2 = (c1 * (1.0 / 24.0 - c1 * (1.0 / 720.0)) - 0.5, c0 * (1.0 / 120.0))
    e = [[None] * 3 for _ in range(3)]
    for k, (d, s) in enumerate(((d0, s0), (d1, s1), (d2, s2))):
        e[k][k] = (q0[0] + q1[0] * d + q2[0] * s, q0[1] + q1[1] * d + q2[1] * s)
    for i, j, o, s in ((0, 1, o01, s01), (0, 2, o02, s02), (1, 2, o12, s12)):
        a_re = q1[0] * o[0] + q2[0] * s[0]
        a_im = q1[0] * o[1] + q2[0] * s[1]
        b_re = q1[1] * o[0] + q2[1] * s[0]
        b_im = q1[1] * o[1] + q2[1] * s[1]
        e[i][j] = (a_re - b_im, a_im + b_re)
        e[j][i] = (a_re + b_im, b_re - a_im)
    return e


def kernel(
    n_xd, n_ta, u_in, m_in, noise, partner, u_out, m_out,
    h0, q0, h2, q2, phi, resp, acc, ahead, moved, f_perm, mom,
    face_out, face_in, time_out, time_in, force_out, force_in,
    face_s, face_r, time_s, time_r, force_s, force_r,
):
    n2 = face_in.shape[-2]
    rows, lanes = phi.shape[-2:]
    x1 = rows // n2
    xd, ta = lax.axis_index("xd"), lax.axis_index("ta")
    up = {"xd": lax.rem(xd + 1, n_xd)}
    down = {"xd": lax.rem(xd + n_xd - 1, n_xd)}
    mirror = {"xd": lax.rem(xd + n_xd // 2, n_xd)}
    later = {"ta": lax.rem(ta + 1, n_ta)}
    earlier = {"ta": lax.rem(ta + n_ta - 1, n_ta)}
    sign_ahead = jnp.where(ta == n_ta - 1, -1.0, 1.0).astype(F32)
    sign_behind = jnp.where(ta == 0, -1.0, 1.0).astype(F32)

    barrier = pltpu.get_barrier_semaphore()
    for other in (up, down, mirror, later, earlier):
        pl.semaphore_signal(barrier, inc=1, device_id=other, device_id_type=MESH)
    pl.semaphore_wait(barrier, 5)

    row = lax.broadcasted_iota(jnp.int32, (rows, lanes), 0)
    x_row = lax.div(row, n2)
    at_first = lax.rem(row, n2) == 0
    at_last = lax.rem(row, n2) == n2 - 1
    source_row = jnp.zeros((rows, lanes), jnp.int32)
    for x in range(x1):
        source_row = jnp.where(x_row == x, lax.rem(partner[x], x1), source_row)
    from_row = [source_row == x for x in range(x1)]
    turn = [source_row == lax.rem(x_row + d, x1) for d in range(x1)]

    def from_mirror(into, k, c):
        shape = into.shape[2:4] + (rows, lanes)
        taken = jnp.broadcast_to(into[k, c, :, :, 0:1], shape)
        for x in range(1, x1):
            other = jnp.broadcast_to(into[k, c, :, :, x : x + 1], shape)
            taken = jnp.where(from_row[x], other, taken)
        return taken

    sent = []
    count = {"face": 0, "time": 0}

    def send(kind, out, into, s_sem, r_sem, k, where):
        copy = pltpu.make_async_remote_copy(
            src_ref=out.at[k], dst_ref=into.at[k], send_sem=s_sem.at[k], recv_sem=r_sem.at[k],
            device_id=where, device_id_type=MESH,
        )
        copy.start()
        sent.append(copy)
        return copy, into, k

    def send_face(where):
        k = count["face"]
        count["face"] += 1
        return send("face", face_out, face_in, face_s, face_r, k, where)

    def send_time(where):
        k = count["time"]
        count["time"] += 1
        return send("time", time_out, time_in, time_s, time_r, k, where)

    def start_ahead(mu, half):
        for c in range(2):
            if mu == 0:
                h0[c, :, :, 0:rows] = half[c]
                face_out[count["face"], c] = half[c][:, :, 0:n2]
            elif mu == 1:
                time_out[count["time"], c] = half[c]
            elif mu == 2:
                h2[c, :, :, 0:rows] = half[c]
                for x in range(x1):
                    face_out[count["face"], c, :, :, x : x + 1] = half[c][:, :, x * n2 : x * n2 + 1]
        if mu == 0:
            return send_face(down)
        if mu == 1:
            return send_time(earlier)
        return send_face(mirror)

    def start_behind(mu, half):
        for c in range(2):
            if mu == 0:
                q0[c, :, :, 8 : 8 + rows] = half[c]
                face_out[count["face"], c] = half[c][:, :, rows - n2 : rows]
            elif mu == 1:
                time_out[count["time"], c] = half[c]
            elif mu == 2:
                q2[c, :, :, 8 : 8 + rows] = half[c]
                for x in range(x1):
                    last = x * n2 + n2 - 1
                    face_out[count["face"], c, :, :, x : x + 1] = half[c][:, :, last : last + 1]
        if mu == 0:
            return send_face(up)
        if mu == 1:
            return send_time(later)
        return send_face(mirror)

    def lane_roll(half, shift):
        return tuple(
            pltpu.roll(part.reshape(-1, lanes), shift, 1).reshape(part.shape) for part in half
        )

    def finish_ahead(mu, started, half=None):
        if mu == 3:
            return lane_roll(half, lanes - 1)
        copy, into, k = started
        copy.wait_recv()
        if mu == 0:
            h0[:, :, :, rows : rows + n2] = into[k]
            return tuple(h0[c, :, :, n2 : n2 + rows] for c in range(2))
        if mu == 1:
            return tuple(into[k, c] * sign_ahead for c in range(2))
        return tuple(
            jnp.where(at_last, from_mirror(into, k, c), h2[c, :, :, 1 : 1 + rows])
            for c in range(2)
        )

    def finish_behind(mu, started, half=None):
        if mu == 3:
            return lane_roll(half, 1)
        copy, into, k = started
        copy.wait_recv()
        if mu == 0:
            q0[:, :, :, 8 - n2 : 8] = into[k]
            return tuple(q0[c, :, :, 8 - n2 : 8 - n2 + rows] for c in range(2))
        if mu == 1:
            return tuple(into[k, c] * sign_behind for c in range(2))
        return tuple(
            jnp.where(at_first, from_mirror(into, k, c), q2[c, :, :, 7 : 7 + rows])
            for c in range(2)
        )

    def add_hop(mu, uh, qh, first):
        order, g_re, g_im = gamma_table[mu]
        total = [uh[c] + qh[c] for c in range(2)]
        diff = [uh[c] - qh[c] for c in range(2)]
        for c in range(2):
            upper = total[c]
            acc[c, 0:2] = upper if first else acc[c, 0:2] + upper
        for s in range(2, 4):
            low = times_i(diff[0][order[s]], diff[1][order[s]], g_re[s], g_im[s])
            for c in range(2):
                acc[c, s] = low[c] if first else acc[c, s] + low[c]

    def finish_spinor(source, out):
        out[...] = source[...] - hopping * acc[...]

    h2[:, :, :, rows : rows + 8] = jnp.zeros_like(h2[:, :, :, rows : rows + 8])
    q2[:, :, :, 0:8] = jnp.zeros_like(q2[:, :, :, 0:8])

    def dirac(source, out, links, keep, have_ahead, behind_ready=None):
        started_h, started_q = {}, {}
        for mu in (1, 2, 0):
            if not have_ahead:
                started_h[mu] = start_ahead(mu, project(source, mu, 1))
            if behind_ready is None:
                started_q[mu] = start_behind(mu, dag_vec(links, mu, project(source, mu, -1)))
            else:
                started_q[mu] = behind_ready[mu]
        first = True
        for mu in (3, 0, 2, 1):
            if have_ahead:
                half = tuple(ahead[mu, c] for c in range(2))
            else:
                half = finish_ahead(
                    mu, started_h.get(mu), project(source, mu, 1) if mu == 3 else None
                )
                if keep:
                    for c in range(2):
                        ahead[mu, c] = half[c]
            uh = mat_vec(links, mu, half)
            if keep:
                for c in range(2):
                    moved[mu, c] = uh[c]
            qh = finish_behind(
                mu, started_q.get(mu),
                dag_vec(links, mu, project(source, mu, -1)) if mu == 3 else None,
            )
            add_hop(mu, uh, qh, first)
            first = False
        finish_spinor(source, out)

    def force(mu, k, links, x_half):
        ux = mat_vec(links, mu, x_half)
        one = outer(ux, project(phi, mu, -1))
        two = outer(tuple(moved[mu, c] for c in range(2)), project(resp, mu, 1))
        g_re, g_im = one[0] + two[0], one[1] + two[1]
        scale = -2.0 * hopping
        third = (g_im[0, 0] + g_im[1, 1] + g_im[2, 2]) * (1.0 / 3.0)
        force_out[k, 0] = scale * (g_im[0, 0] - third)
        force_out[k, 1] = scale * (g_im[1, 1] - third)
        for n, (i, j) in enumerate(((0, 1), (0, 2), (1, 2))):
            force_out[k, 2 + 2 * n] = (0.5 * scale) * (g_im[i, j] + g_im[j, i])
            force_out[k, 3 + 2 * n] = (0.5 * scale) * (g_re[j, i] - g_re[i, j])
        return send("force", force_out, force_in, force_s, force_r, k, mirror)

    def update(mu, k, started, links, last):
        started[0].wait_recv()
        f_perm[:, 0:rows] = force_in[k]
        f_perm[:, rows : 2 * rows] = force_in[k]
        mirrored = f_perm[:, 0:rows]
        for d in range(1, x1):
            mirrored = jnp.where(turn[d], f_perm[:, d * n2 : d * n2 + rows], mirrored)
        p = []
        for n in range(8):
            real = n < 2 or n % 2 == 0
            here, there = force_out[k, n], mirrored[n]
            p.append(mom[mu, n] + step_size * (here - there if real else here + there))
        if last:
            zero = jnp.zeros((rows, lanes), F32)
            for n in range(3):
                m_out[mu, 0, n, n] = p[n] if n < 2 else -(p[0] + p[1])
                m_out[mu, 1, n, n] = zero
            for n, (i, j) in enumerate(((0, 1), (0, 2), (1, 2))):
                m_out[mu, 0, i, j] = p[2 + 2 * n]
                m_out[mu, 0, j, i] = p[2 + 2 * n]
                m_out[mu, 1, i, j] = p[3 + 2 * n]
                m_out[mu, 1, j, i] = -p[3 + 2 * n]
        else:
            for n in range(8):
                mom[mu, n] = p[n]
        e = link_exponential(p)
        u = [[(links[mu, 0, i, j], links[mu, 1, i, j]) for j in range(3)] for i in range(3)]
        for i in range(3):
            for j in range(3):
                parts = [complex_times(e[i][k2], u[k2][j]) for k2 in range(3)]
                for c in range(2):
                    u_out[mu, c, i, j] = parts[0][c] + parts[1][c] + parts[2][c]

    for mu in range(4):
        mom[mu, 0] = m_in[mu, 0, 0, 0]
        mom[mu, 1] = m_in[mu, 0, 1, 1]
        for n, (i, j) in enumerate(((0, 1), (0, 2), (1, 2))):
            mom[mu, 2 + 2 * n] = m_in[mu, 0, i, j]
            mom[mu, 3 + 2 * n] = m_in[mu, 1, i, j]

    dirac(noise, phi, u_in, False, False)
    behind_ready = None
    for step in range(MD_STEPS):
        links = u_in if step == 0 else u_out
        last = step == MD_STEPS - 1
        dirac(phi, resp, links, True, step > 0, behind_ready)
        started = {mu: start_ahead(mu, project(resp, mu, -1)) for mu in (1, 2, 0)}
        forces = {}
        for mu in (3, 0, 2, 1):
            x_half = finish_ahead(
                mu, started.get(mu), project(resp, mu, -1) if mu == 3 else None
            )
            forces[mu] = force(mu, 4 * step + mu, links, x_half)
        behind_ready = {}
        for mu in (3, 0, 2, 1):
            update(mu, 4 * step + mu, forces[mu], links, last)
            if not last and mu != 3:
                behind_ready[mu] = start_behind(mu, dag_vec(u_out, mu, project(phi, mu, -1)))
    for copy in sent:
        copy.wait_send()


def per_device(gauge_links, momenta, noise_table, noise_index, partner):
    lead = gauge_links.shape[:4]
    x1, n2, n3 = gauge_links.shape[4], gauge_links.shape[6], gauge_links.shape[7]
    rows = x1 * n2
    n_xd, n_ta = lax.axis_size("xd"), lax.axis_size("ta")
    noise = pl.pallas_call(
        noise_kernel,
        out_shape=jax.ShapeDtypeStruct((8, 3, rows, n3), F32),
    )(noise_table.reshape((8,) + noise_table.shape[2:]), noise_index.reshape(rows, n3))
    noise = noise.reshape(2, 4, 3, rows, n3)
    vmem = pl.BlockSpec(memory_space=pltpu.VMEM)
    half = (2, 2, 3)
    faces = 8 + 2 * MD_STEPS + 2 * (MD_STEPS - 1)
    times = 4 + MD_STEPS + (MD_STEPS - 1)
    field = (2, 4, 3, rows, n3)
    full = jax.ShapeDtypeStruct(lead + (rows, n3), F32)
    dma = pltpu.SemaphoreType.DMA
    new_links, new_momenta = pl.pallas_call(
        functools.partial(kernel, n_xd, n_ta),
        out_shape=(full, full),
        in_specs=[vmem, vmem, vmem, pl.BlockSpec(memory_space=pltpu.SMEM)],
        out_specs=(vmem, vmem),
        scratch_shapes=[
            pltpu.VMEM(half + (rows + 8, n3), F32),
            pltpu.VMEM(half + (rows + 8, n3), F32),
            pltpu.VMEM(half + (rows + 8, n3), F32),
            pltpu.VMEM(half + (rows + 8, n3), F32),
            pltpu.VMEM(field, F32),
            pltpu.VMEM(field, F32),
            pltpu.VMEM(field, F32),
            pltpu.VMEM((4,) + half + (rows, n3), F32),
            pltpu.VMEM((4,) + half + (rows, n3), F32),
            pltpu.VMEM((8, 2 * rows, n3), F32),
            pltpu.VMEM((4, 8, rows, n3), F32),
            pltpu.VMEM((faces,) + half + (n2, n3), F32),
            pltpu.VMEM((faces,) + half + (n2, n3), F32),
            pltpu.VMEM((times,) + half + (rows, n3), F32),
            pltpu.VMEM((times,) + half + (rows, n3), F32),
            pltpu.VMEM((4 * MD_STEPS, 8, rows, n3), F32),
            pltpu.VMEM((4 * MD_STEPS, 8, rows, n3), F32),
            dma((faces,)), dma((faces,)), dma((times,)), dma((times,)),
            dma((4 * MD_STEPS,)), dma((4 * MD_STEPS,)),
        ],
        compiler_params=pltpu.CompilerParams(
            collective_id=0, has_side_effects=True, vmem_limit_bytes=40 * 1024 * 1024
        ),
    )(
        gauge_links.reshape(lead + (rows, n3)), momenta.reshape(lead + (rows, n3)), noise, partner
    )
    return new_links.reshape(gauge_links.shape), new_momenta.reshape(momenta.shape)


def solution(mesh):
    placed = (
        P(None, None, None, None, "xd", "ta", None, None),
        P(None, None, None, None, "xd", "ta", None, None),
        P(),
        P("xd", "ta", None, None),
        P("xd"),
    )
    return jax.shard_map(
        per_device,
        mesh=mesh,
        in_specs=placed,
        out_specs=(
            P(None, None, None, None, "xd", "ta", None, None),
            P(None, None, None, None, "xd", "ta", None, None),
        ),
        check_vma=False,
    )
```

```python
import functools

import jax
import jax.numpy as jnp
from jax import lax
from jax.experimental import pallas as pl
from jax.experimental.pallas import tpu as pltpu
from jax.sharding import PartitionSpec as P

MESH = pl.DeviceIdType.MESH
F32 = jnp.float32

MD_STEPS = 2

hopping = 0.13
step_size = 0.25
gamma_table = (
    ((3, 2, 1, 0), (0, 0, 0, 0), (1, 1, -1, -1)),
    ((2, 3, 0, 1), (1, 1, 1, 1), (0, 0, 0, 0)),
    ((3, 2, 1, 0), (-1, 1, 1, -1), (0, 0, 0, 0)),
    ((2, 3, 0, 1), (0, 0, 0, 0), (1, -1, -1, 1)),
)


def gather_noise(table, index, out):
    rows, lanes = index.shape
    entries = table.shape[-1]
    lane = jnp.bitwise_and(index[...], lanes - 1)
    chunk = lax.div(index[...], lanes)

    def one(k, carry):
        part, colour = lax.div(k, 3), lax.rem(k, 3)
        for spin in range(4):
            total = jnp.zeros((rows, lanes), F32)
            for c in range(entries // lanes):
                row = table[part, colour, spin : spin + 1, c * lanes : (c + 1) * lanes]
                value = jnp.take_along_axis(
                    jnp.broadcast_to(row, (rows, lanes)), lane, axis=1, mode="promise_in_bounds"
                )
                total = jnp.where(chunk == c, value, total)
            out[part, spin, colour] = total
        return carry

    lax.fori_loop(0, 6, one, 0)


def times_i(re, im, g_re, g_im):
    if g_re == 1:
        return re, im
    if g_re == -1:
        return -re, -im
    if g_im == 1:
        return -im, re
    return im, -re


def project(spinor, mu, sign):
    order, g_re, g_im = gamma_table[mu]
    out_re, out_im = [], []
    for s in range(2):
        add_re, add_im = times_i(
            spinor[0, order[s]], spinor[1, order[s]], sign * g_re[s], sign * g_im[s]
        )
        out_re.append(spinor[0, s] + add_re)
        out_im.append(spinor[1, s] + add_im)
    return jnp.stack(out_re), jnp.stack(out_im)


def mat_vec(links, mu, half):
    re, im = half
    out_re = out_im = None
    for b in range(3):
        m_re, m_im = links[mu, 0, :, b][None], links[mu, 1, :, b][None]
        v_re, v_im = re[:, b : b + 1], im[:, b : b + 1]
        t_re = m_re * v_re - m_im * v_im
        t_im = m_re * v_im + m_im * v_re
        out_re = t_re if b == 0 else out_re + t_re
        out_im = t_im if b == 0 else out_im + t_im
    return out_re, out_im


def dag_vec(links, mu, half):
    re, im = half
    out_re = out_im = None
    for b in range(3):
        m_re, m_im = links[mu, 0, b][None], links[mu, 1, b][None]
        v_re, v_im = re[:, b : b + 1], im[:, b : b + 1]
        t_re = m_re * v_re + m_im * v_im
        t_im = m_re * v_im - m_im * v_re
        out_re = t_re if b == 0 else out_re + t_re
        out_im = t_im if b == 0 else out_im + t_im
    return out_re, out_im


def outer(first, second):
    out_re = out_im = None
    for s in range(2):
        f_re, f_im = first[0][s][:, None], first[1][s][:, None]
        g_re, g_im = second[0][s][None], second[1][s][None]
        t_re = f_re * g_re + f_im * g_im
        t_im = f_im * g_re - f_re * g_im
        out_re = t_re if s == 0 else out_re + t_re
        out_im = t_im if s == 0 else out_im + t_im
    return out_re, out_im


def complex_times(a, b):
    return a[0] * b[0] - a[1] * b[1], a[0] * b[1] + a[1] * b[0]


def complex_by_conj(a, b):
    return a[0] * b[0] + a[1] * b[1], a[1] * b[0] - a[0] * b[1]


def square(c):
    return c[0] * c[0] + c[1] * c[1]


def link_exponential(p):
    b = [step_size * part for part in p]
    d0, d1 = b[0], b[1]
    d2 = -(d0 + d1)
    o01, o02, o12 = (b[2], b[3]), (b[4], b[5]), (b[6], b[7])
    n01, n02, n12 = square(o01), square(o02), square(o12)
    s0 = d0 * d0 + n01 + n02
    s1 = d1 * d1 + n01 + n12
    s2 = d2 * d2 + n02 + n12
    r01 = complex_by_conj(o02, o12)
    r02 = complex_times(o01, o12)
    r12 = complex_times((o01[0], -o01[1]), o02)
    s01 = (r01[0] - d2 * o01[0], r01[1] - d2 * o01[1])
    s02 = (r02[0] - d1 * o02[0], r02[1] - d1 * o02[1])
    s12 = (r12[0] - d0 * o12[0], r12[1] - d0 * o12[1])
    c1 = 0.5 * (s0 + s1 + s2)
    c0 = (
        d0 * (d1 * d2 - n12) - d1 * n02 - d2 * n01
        + 2.0 * (r02[0] * o02[0] + r02[1] * o02[1])
    )
    q0 = (1.0 - c0 * c0 * (1.0 / 720.0), c0 * (c1 * (1.0 / 120.0) - 1.0 / 6.0))
    q1 = (c0 * (1.0 / 24.0 - c1 * (1.0 / 360.0)), 1.0 + c1 * (c1 * (1.0 / 120.0) - 1.0 / 6.0))
    q2 = (c1 * (1.0 / 24.0 - c1 * (1.0 / 720.0)) - 0.5, c0 * (1.0 / 120.0))
    e = [[None] * 3 for _ in range(3)]
    for k, (d, s) in enumerate(((d0, s0), (d1, s1), (d2, s2))):
        e[k][k] = (q0[0] + q1[0] * d + q2[0] * s, q0[1] + q1[1] * d + q2[1] * s)
    for i, j, o, s in ((0, 1, o01, s01), (0, 2, o02, s02), (1, 2, o12, s12)):
        a_re = q1[0] * o[0] + q2[0] * s[0]
        a_im = q1[0] * o[1] + q2[0] * s[1]
        b_re = q1[1] * o[0] + q2[1] * s[0]
        b_im = q1[1] * o[1] + q2[1] * s[1]
        e[i][j] = (a_re - b_im, a_im + b_re)
        e[j][i] = (a_re + b_im, b_re - a_im)
    return e


def kernel(
    n_xd, n_ta, u_hbm, m_hbm, table, index, partner, u_out, m_out,
    u_in, m_in, noise,
    h0, q0, h2, q2, phi, resp, acc, ahead, moved, f_perm, mom,
    face_out, face_in, time_out, time_in, force_out, force_in,
    face_s, face_r, time_s, time_r, force_s, force_r, load_s,
):
    n2 = face_in.shape[-2]
    rows, lanes = phi.shape[-2:]
    x1 = rows // n2
    xd, ta = lax.axis_index("xd"), lax.axis_index("ta")
    up = {"xd": lax.rem(xd + 1, n_xd)}
    down = {"xd": lax.rem(xd + n_xd - 1, n_xd)}
    mirror = {"xd": lax.rem(xd + n_xd // 2, n_xd)}
    later = {"ta": lax.rem(ta + 1, n_ta)}
    earlier = {"ta": lax.rem(ta + n_ta - 1, n_ta)}
    sign_ahead = jnp.where(ta == n_ta - 1, -1.0, 1.0).astype(F32)
    sign_behind = jnp.where(ta == 0, -1.0, 1.0).astype(F32)

    barrier = pltpu.get_barrier_semaphore()
    for other in (up, down, mirror, later, earlier):
        pl.semaphore_signal(barrier, inc=1, device_id=other, device_id_type=MESH)
    loads = [
        pltpu.make_async_copy(u_hbm, u_in, load_s.at[0]),
        pltpu.make_async_copy(m_hbm, m_in, load_s.at[1]),
    ]
    for load in loads:
        load.start()
    gather_noise(table, index, noise)
    pl.semaphore_wait(barrier, 5)
    loads[0].wait()

    row = lax.broadcasted_iota(jnp.int32, (rows, lanes), 0)
    x_row = lax.div(row, n2)
    at_first = lax.rem(row, n2) == 0
    at_last = lax.rem(row, n2) == n2 - 1
    source_row = jnp.zeros((rows, lanes), jnp.int32)
    for x in range(x1):
        source_row = jnp.where(x_row == x, lax.rem(partner[x], x1), source_row)
    from_row = [source_row == x for x in range(x1)]
    turn = [source_row == lax.rem(x_row + d, x1) for d in range(x1)]

    def from_mirror(into, k, c):
        shape = into.shape[2:4] + (rows, lanes)
        taken = jnp.broadcast_to(into[k, c, :, :, 0:1], shape)
        for x in range(1, x1):
            other = jnp.broadcast_to(into[k, c, :, :, x : x + 1], shape)
            taken = jnp.where(from_row[x], other, taken)
        return taken

    sent = []
    count = {"face": 0, "time": 0}

    def send(kind, out, into, s_sem, r_sem, k, where):
        copy = pltpu.make_async_remote_copy(
            src_ref=out.at[k], dst_ref=into.at[k], send_sem=s_sem.at[k], recv_sem=r_sem.at[k],
            device_id=where, device_id_type=MESH,
        )
        copy.start()
        sent.append(copy)
        return copy, into, k

    def send_face(where):
        k = count["face"]
        count["face"] += 1
        return send("face", face_out, face_in, face_s, face_r, k, where)

    def send_time(where):
        k = count["time"]
        count["time"] += 1
        return send("time", time_out, time_in, time_s, time_r, k, where)

    def start_ahead(mu, half):
        for c in range(2):
            if mu == 0:
                h0[c, :, :, 0:rows] = half[c]
                face_out[count["face"], c] = half[c][:, :, 0:n2]
            elif mu == 1:
                time_out[count["time"], c] = half[c]
            elif mu == 2:
                h2[c, :, :, 0:rows] = half[c]
                for x in range(x1):
                    face_out[count["face"], c, :, :, x : x + 1] = half[c][:, :, x * n2 : x * n2 + 1]
        if mu == 0:
            return send_face(down)
        if mu == 1:
            return send_time(earlier)
        return send_face(mirror)

    def start_behind(mu, half):
        for c in range(2):
            if mu == 0:
                q0[c, :, :, 8 : 8 + rows] = half[c]
                face_out[count["face"], c] = half[c][:, :, rows - n2 : rows]
            elif mu == 1:
                time_out[count["time"], c] = half[c]
            elif mu == 2:
                q2[c, :, :, 8 : 8 + rows] = half[c]
                for x in range(x1):
                    last = x * n2 + n2 - 1
                    face_out[count["face"], c, :, :, x : x + 1] = half[c][:, :, last : last + 1]
        if mu == 0:
            return send_face(up)
        if mu == 1:
            return send_time(later)
        return send_face(mirror)

    def lane_roll(half, shift):
        return tuple(
            pltpu.roll(part.reshape(-1, lanes), shift, 1).reshape(part.shape) for part in half
        )

    def finish_ahead(mu, started, half=None):
        if mu == 3:
            return lane_roll(half, lanes - 1)
        copy, into, k = started
        copy.wait_recv()
        if mu == 0:
            h0[:, :, :, rows : rows + n2] = into[k]
            return tuple(h0[c, :, :, n2 : n2 + rows] for c in range(2))
        if mu == 1:
            return tuple(into[k, c] * sign_ahead for c in range(2))
        return tuple(
            jnp.where(at_last, from_mirror(into, k, c), h2[c, :, :, 1 : 1 + rows])
            for c in range(2)
        )

    def finish_behind(mu, started, half=None):
        if mu == 3:
            return lane_roll(half, 1)
        copy, into, k = started
        copy.wait_recv()
        if mu == 0:
            q0[:, :, :, 8 - n2 : 8] = into[k]
            return tuple(q0[c, :, :, 8 - n2 : 8 - n2 + rows] for c in range(2))
        if mu == 1:
            return tuple(into[k, c] * sign_behind for c in range(2))
        return tuple(
            jnp.where(at_first, from_mirror(into, k, c), q2[c, :, :, 7 : 7 + rows])
            for c in range(2)
        )

    def add_hop(mu, half, sign, first=False):
        order, g_re, g_im = gamma_table[mu]
        for c in range(2):
            acc[c, 0:2] = half[c] if first else acc[c, 0:2] + half[c]
        for s in range(2, 4):
            low = times_i(half[0][order[s]], half[1][order[s]], sign * g_re[s], sign * g_im[s])
            for c in range(2):
                acc[c, s] = low[c] if first else acc[c, s] + low[c]

    def finish_spinor(source, out):
        out[...] = source[...] - hopping * acc[...]

    h2[:, :, :, rows : rows + 8] = jnp.zeros_like(h2[:, :, :, rows : rows + 8])
    q2[:, :, :, 0:8] = jnp.zeros_like(q2[:, :, :, 0:8])

    def local_hop(links, source, mu, half, keep, first):
        uh = mat_vec(links, mu, half)
        if keep:
            for c in range(2):
                moved[mu, c] = uh[c]
        add_hop(mu, uh, 1, first)

    def dirac(source, out, links, keep):
        started_h, started_q = {}, {}
        for mu in (2, 1, 0):
            started_h[mu] = start_ahead(mu, project(source, mu, 1))
            started_q[mu] = start_behind(mu, dag_vec(links, mu, project(source, mu, -1)))
        for mu in (3, 0, 1, 2):
            half = finish_ahead(mu, started_h.get(mu), project(source, mu, 1) if mu == 3 else None)
            if keep:
                for c in range(2):
                    ahead[mu, c] = half[c]
            local_hop(links, source, mu, half, keep, mu == 3)
            qh = dag_vec(links, mu, project(source, mu, -1)) if mu == 3 else None
            add_hop(mu, finish_behind(mu, started_q.get(mu), qh), -1)
        finish_spinor(source, out)

    early = 6

    def force(mu, k, links, x_half):
        ux = mat_vec(links, mu, x_half)
        one = outer(ux, project(phi, mu, -1))
        two = outer(tuple(moved[mu, c] for c in range(2)), project(resp, mu, 1))
        g_re, g_im = one[0] + two[0], one[1] + two[1]
        scale = -2.0 * hopping
        third = (g_im[0, 0] + g_im[1, 1] + g_im[2, 2]) * (1.0 / 3.0)
        force_out[k, 0] = scale * (g_im[0, 0] - third)
        force_out[k, 1] = scale * (g_im[1, 1] - third)
        for n, (i, j) in enumerate(((0, 1), (0, 2), (1, 2))):
            force_out[k, 2 + 2 * n] = (0.5 * scale) * (g_im[i, j] + g_im[j, i])
            force_out[k, 3 + 2 * n] = (0.5 * scale) * (g_re[j, i] - g_re[i, j])

    def send_force(k, piece):
        rows_of = (pl.ds(0, early), pl.ds(early, 8 - early), pl.ds(0, 8))[piece]
        copy = pltpu.make_async_remote_copy(
            src_ref=force_out.at[k, rows_of], dst_ref=force_in.at[k, rows_of],
            send_sem=force_s.at[k, piece], recv_sem=force_r.at[k, piece],
            device_id=mirror, device_id_type=MESH,
        )
        copy.start()
        sent.append(copy)
        return copy

    def update(mu, k, started, links, last):
        for copy in started:
            copy.wait_recv()
        f_perm[:, 0:rows] = force_in[k]
        f_perm[:, rows : 2 * rows] = force_in[k]
        mirrored = f_perm[:, 0:rows]
        for d in range(1, x1):
            mirrored = jnp.where(turn[d], f_perm[:, d * n2 : d * n2 + rows], mirrored)
        p = []
        for n in range(8):
            real = n < 2 or n % 2 == 0
            here, there = force_out[k, n], mirrored[n]
            p.append(mom[mu, n] + step_size * (here - there if real else here + there))
        if last:
            zero = jnp.zeros((rows, lanes), F32)
            for n in range(3):
                m_out[mu, 0, n, n] = p[n] if n < 2 else -(p[0] + p[1])
                m_out[mu, 1, n, n] = zero
            for n, (i, j) in enumerate(((0, 1), (0, 2), (1, 2))):
                m_out[mu, 0, i, j] = p[2 + 2 * n]
                m_out[mu, 0, j, i] = p[2 + 2 * n]
                m_out[mu, 1, i, j] = p[3 + 2 * n]
                m_out[mu, 1, j, i] = -p[3 + 2 * n]
        else:
            for n in range(8):
                mom[mu, n] = p[n]
        e = link_exponential(p)
        u = [[(links[mu, 0, i, j], links[mu, 1, i, j]) for j in range(3)] for i in range(3)]
        for i in range(3):
            for j in range(3):
                parts = [complex_times(e[i][k2], u[k2][j]) for k2 in range(3)]
                for c in range(2):
                    u_out[mu, c, i, j] = parts[0][c] + parts[1][c] + parts[2][c]

    dirac(noise, phi, u_in, False)
    dirac(phi, resp, u_in, True)
    loads[1].wait()
    for mu in range(4):
        mom[mu, 0] = m_in[mu, 0, 0, 0]
        mom[mu, 1] = m_in[mu, 0, 1, 1]
        for n, (i, j) in enumerate(((0, 1), (0, 2), (1, 2))):
            mom[mu, 2 + 2 * n] = m_in[mu, 0, i, j]
            mom[mu, 3 + 2 * n] = m_in[mu, 1, i, j]
    for step in range(MD_STEPS):
        links = u_in if step == 0 else u_out
        last = step == MD_STEPS - 1
        started = {mu: start_ahead(mu, project(resp, mu, -1)) for mu in (2, 1, 0)}
        forces = {}
        for mu in (3, 0, 1, 2):
            x_half = finish_ahead(
                mu, started.get(mu), project(resp, mu, -1) if mu == 3 else None
            )
            force(mu, 4 * step + mu, links, x_half)
            forces[mu] = [send_force(4 * step + mu, 0 if mu == 3 else 2)]
        forces[3].append(send_force(4 * step + 3, 1))
        behind = {}
        for mu in (0, 1, 2, 3):
            update(mu, 4 * step + mu, forces[mu], links, last)
            if last:
                continue
            qh = dag_vec(u_out, mu, project(phi, mu, -1))
            if mu != 3:
                behind[mu] = start_behind(mu, qh)
            else:
                add_hop(mu, finish_behind(mu, None, qh), -1)
            half = tuple(ahead[mu, c] for c in range(2))
            local_hop(u_out, phi, mu, half, True, mu == 0)
        if not last:
            for mu in (0, 1, 2):
                add_hop(mu, finish_behind(mu, behind[mu]), -1)
            finish_spinor(phi, resp)
    for copy in sent:
        copy.wait_send()


def per_device(gauge_links, momenta, noise_table, noise_index, partner):
    lead = gauge_links.shape[:4]
    x1, n2, n3 = gauge_links.shape[4], gauge_links.shape[6], gauge_links.shape[7]
    rows = x1 * n2
    n_xd, n_ta = lax.axis_size("xd"), lax.axis_size("ta")
    vmem = pl.BlockSpec(memory_space=pltpu.VMEM)
    hbm = pl.BlockSpec(memory_space=pltpu.HBM)
    half = (2, 2, 3)
    faces = 8 + 2 * MD_STEPS + 2 * (MD_STEPS - 1)
    times = 4 + MD_STEPS + (MD_STEPS - 1)
    field = (2, 4, 3, rows, n3)
    full = jax.ShapeDtypeStruct(lead + (rows, n3), F32)
    dma = pltpu.SemaphoreType.DMA
    new_links, new_momenta = pl.pallas_call(
        functools.partial(kernel, n_xd, n_ta),
        out_shape=(full, full),
        in_specs=[hbm, hbm, vmem, vmem, pl.BlockSpec(memory_space=pltpu.SMEM)],
        out_specs=(vmem, vmem),
        scratch_shapes=[
            pltpu.VMEM(lead + (rows, n3), F32),
            pltpu.VMEM(lead + (rows, n3), F32),
            pltpu.VMEM(field, F32),
            pltpu.VMEM(half + (rows + 8, n3), F32),
            pltpu.VMEM(half + (rows + 8, n3), F32),
            pltpu.VMEM(half + (rows + 8, n3), F32),
            pltpu.VMEM(half + (rows + 8, n3), F32),
            pltpu.VMEM(field, F32),
            pltpu.VMEM(field, F32),
            pltpu.VMEM(field, F32),
            pltpu.VMEM((4,) + half + (rows, n3), F32),
            pltpu.VMEM((4,) + half + (rows, n3), F32),
            pltpu.VMEM((8, 2 * rows, n3), F32),
            pltpu.VMEM((4, 8, rows, n3), F32),
            pltpu.VMEM((faces,) + half + (n2, n3), F32),
            pltpu.VMEM((faces,) + half + (n2, n3), F32),
            pltpu.VMEM((times,) + half + (rows, n3), F32),
            pltpu.VMEM((times,) + half + (rows, n3), F32),
            pltpu.VMEM((4 * MD_STEPS, 8, rows, n3), F32),
            pltpu.VMEM((4 * MD_STEPS, 8, rows, n3), F32),
            dma((faces,)), dma((faces,)), dma((times,)), dma((times,)),
            dma((4 * MD_STEPS, 3)), dma((4 * MD_STEPS, 3)),
            dma((2,)),
        ],
        compiler_params=pltpu.CompilerParams(
            collective_id=0, has_side_effects=True, vmem_limit_bytes=40 * 1024 * 1024
        ),
    )(
        gauge_links.reshape(lead + (rows, n3)), momenta.reshape(lead + (rows, n3)),
        jnp.swapaxes(noise_table, 1, 2), noise_index.reshape(rows, n3), partner,
    )
    return new_links.reshape(gauge_links.shape), new_momenta.reshape(momenta.shape)


def solution(mesh):
    placed = (
        P(None, None, None, None, "xd", "ta", None, None),
        P(None, None, None, None, "xd", "ta", None, None),
        P(),
        P("xd", "ta", None, None),
        P("xd"),
    )
    return jax.shard_map(
        per_device,
        mesh=mesh,
        in_specs=placed,
        out_specs=(
            P(None, None, None, None, "xd", "ta", None, None),
            P(None, None, None, None, "xd", "ta", None, None),
        ),
        check_vma=False,
    )
```

```python
import functools

import jax
import jax.numpy as jnp
from jax import lax
from jax.experimental import pallas as pl
from jax.experimental.pallas import tpu as pltpu
from jax.sharding import PartitionSpec as P

MESH = pl.DeviceIdType.MESH
F32 = jnp.float32

MD_STEPS = 2

hopping = 0.13
step_size = 0.25
gamma_table = (
    ((3, 2, 1, 0), (0, 0, 0, 0), (1, 1, -1, -1)),
    ((2, 3, 0, 1), (1, 1, 1, 1), (0, 0, 0, 0)),
    ((3, 2, 1, 0), (-1, 1, 1, -1), (0, 0, 0, 0)),
    ((2, 3, 0, 1), (0, 0, 0, 0), (1, -1, -1, 1)),
)


def gather_noise(table, index, out):
    rows, lanes = index.shape
    entries = table.shape[-1]
    lane = jnp.bitwise_and(index[...], lanes - 1)
    chunk = lax.div(index[...], lanes)

    def one(k, carry):
        part, colour = lax.div(k, 3), lax.rem(k, 3)
        for spin in range(4):
            total = jnp.zeros((rows, lanes), F32)
            for c in range(entries // lanes):
                row = table[part, colour, spin : spin + 1, c * lanes : (c + 1) * lanes]
                value = jnp.take_along_axis(
                    jnp.broadcast_to(row, (rows, lanes)), lane, axis=1, mode="promise_in_bounds"
                )
                total = jnp.where(chunk == c, value, total)
            out[part, spin, colour] = total
        return carry

    lax.fori_loop(0, 6, one, 0)


def times_i(re, im, g_re, g_im):
    if g_re == 1:
        return re, im
    if g_re == -1:
        return -re, -im
    if g_im == 1:
        return -im, re
    return im, -re


def project(spinor, mu, sign):
    order, g_re, g_im = gamma_table[mu]
    out_re, out_im = [], []
    for s in range(2):
        add_re, add_im = times_i(
            spinor[0, order[s]], spinor[1, order[s]], sign * g_re[s], sign * g_im[s]
        )
        out_re.append(spinor[0, s] + add_re)
        out_im.append(spinor[1, s] + add_im)
    return jnp.stack(out_re), jnp.stack(out_im)


def mat_vec(links, mu, half):
    re, im = half
    out_re = out_im = None
    for b in range(3):
        m_re, m_im = links[mu, 0, :, b][None], links[mu, 1, :, b][None]
        v_re, v_im = re[:, b : b + 1], im[:, b : b + 1]
        t_re = m_re * v_re - m_im * v_im
        t_im = m_re * v_im + m_im * v_re
        out_re = t_re if b == 0 else out_re + t_re
        out_im = t_im if b == 0 else out_im + t_im
    return out_re, out_im


def dag_vec(links, mu, half):
    re, im = half
    out_re = out_im = None
    for b in range(3):
        m_re, m_im = links[mu, 0, b][None], links[mu, 1, b][None]
        v_re, v_im = re[:, b : b + 1], im[:, b : b + 1]
        t_re = m_re * v_re + m_im * v_im
        t_im = m_re * v_im - m_im * v_re
        out_re = t_re if b == 0 else out_re + t_re
        out_im = t_im if b == 0 else out_im + t_im
    return out_re, out_im


def outer(first, second):
    out_re = out_im = None
    for s in range(2):
        f_re, f_im = first[0][s][:, None], first[1][s][:, None]
        g_re, g_im = second[0][s][None], second[1][s][None]
        t_re = f_re * g_re + f_im * g_im
        t_im = f_im * g_re - f_re * g_im
        out_re = t_re if s == 0 else out_re + t_re
        out_im = t_im if s == 0 else out_im + t_im
    return out_re, out_im


def complex_times(a, b):
    return a[0] * b[0] - a[1] * b[1], a[0] * b[1] + a[1] * b[0]


def complex_by_conj(a, b):
    return a[0] * b[0] + a[1] * b[1], a[1] * b[0] - a[0] * b[1]


def square(c):
    return c[0] * c[0] + c[1] * c[1]


def link_exponential(p):
    b = [step_size * part for part in p]
    d0, d1 = b[0], b[1]
    d2 = -(d0 + d1)
    o01, o02, o12 = (b[2], b[3]), (b[4], b[5]), (b[6], b[7])
    n01, n02, n12 = square(o01), square(o02), square(o12)
    s0 = d0 * d0 + n01 + n02
    s1 = d1 * d1 + n01 + n12
    s2 = d2 * d2 + n02 + n12
    r01 = complex_by_conj(o02, o12)
    r02 = complex_times(o01, o12)
    r12 = complex_times((o01[0], -o01[1]), o02)
    s01 = (r01[0] - d2 * o01[0], r01[1] - d2 * o01[1])
    s02 = (r02[0] - d1 * o02[0], r02[1] - d1 * o02[1])
    s12 = (r12[0] - d0 * o12[0], r12[1] - d0 * o12[1])
    c1 = 0.5 * (s0 + s1 + s2)
    c0 = (
        d0 * (d1 * d2 - n12) - d1 * n02 - d2 * n01
        + 2.0 * (r02[0] * o02[0] + r02[1] * o02[1])
    )
    q0 = (1.0 - c0 * c0 * (1.0 / 720.0), c0 * (c1 * (1.0 / 120.0) - 1.0 / 6.0))
    q1 = (c0 * (1.0 / 24.0 - c1 * (1.0 / 360.0)), 1.0 + c1 * (c1 * (1.0 / 120.0) - 1.0 / 6.0))
    q2 = (c1 * (1.0 / 24.0 - c1 * (1.0 / 720.0)) - 0.5, c0 * (1.0 / 120.0))
    e = [[None] * 3 for _ in range(3)]
    for k, (d, s) in enumerate(((d0, s0), (d1, s1), (d2, s2))):
        e[k][k] = (q0[0] + q1[0] * d + q2[0] * s, q0[1] + q1[1] * d + q2[1] * s)
    for i, j, o, s in ((0, 1, o01, s01), (0, 2, o02, s02), (1, 2, o12, s12)):
        a_re = q1[0] * o[0] + q2[0] * s[0]
        a_im = q1[0] * o[1] + q2[0] * s[1]
        b_re = q1[1] * o[0] + q2[1] * s[0]
        b_im = q1[1] * o[1] + q2[1] * s[1]
        e[i][j] = (a_re - b_im, a_im + b_re)
        e[j][i] = (a_re + b_im, b_re - a_im)
    return e


def kernel(
    n_xd, n_ta, u_hbm, m_hbm, table_hbm, index_hbm, partner, u_final, m_final,
    u_in, m_in, table, index, u_out, m_out, noise,
    h0, q0, h2, q2, phi, resp, acc, ahead, moved, f_perm, mom,
    face_out, face_in, time_out, time_in, force_out, force_in,
    face_s, face_r, time_s, time_r, force_s, force_r, load_s, store_s,
):
    n2 = face_in.shape[-2]
    rows, lanes = phi.shape[-2:]
    x1 = rows // n2
    xd, ta = lax.axis_index("xd"), lax.axis_index("ta")
    up = {"xd": lax.rem(xd + 1, n_xd)}
    down = {"xd": lax.rem(xd + n_xd - 1, n_xd)}
    mirror = {"xd": lax.rem(xd + n_xd // 2, n_xd)}
    later = {"ta": lax.rem(ta + 1, n_ta)}
    earlier = {"ta": lax.rem(ta + n_ta - 1, n_ta)}
    sign_ahead = jnp.where(ta == n_ta - 1, -1.0, 1.0).astype(F32)
    sign_behind = jnp.where(ta == 0, -1.0, 1.0).astype(F32)

    loads = [
        pltpu.make_async_copy(u_hbm, u_in, load_s.at[0]),
        pltpu.make_async_copy(m_hbm, m_in, load_s.at[1]),
        pltpu.make_async_copy(table_hbm, table, load_s.at[2]),
        pltpu.make_async_copy(index_hbm, index, load_s.at[3]),
    ]
    for n in (3, 2, 0, 1):
        loads[n].start()
    barrier = pltpu.get_barrier_semaphore()
    for other in (up, down, mirror, later, earlier):
        pl.semaphore_signal(barrier, inc=1, device_id=other, device_id_type=MESH)
    loads[3].wait()
    loads[2].wait()
    gather_noise(table, index, noise)
    pl.semaphore_wait(barrier, 5)
    loads[0].wait()

    row = lax.broadcasted_iota(jnp.int32, (rows, lanes), 0)
    x_row = lax.div(row, n2)
    at_first = lax.rem(row, n2) == 0
    at_last = lax.rem(row, n2) == n2 - 1
    source_row = jnp.zeros((rows, lanes), jnp.int32)
    for x in range(x1):
        source_row = jnp.where(x_row == x, lax.rem(partner[x], x1), source_row)
    from_row = [source_row == x for x in range(x1)]
    turn = [source_row == lax.rem(x_row + d, x1) for d in range(x1)]

    def from_mirror(into, k, c):
        shape = into.shape[2:4] + (rows, lanes)
        taken = jnp.broadcast_to(into[k, c, :, :, 0:1], shape)
        for x in range(1, x1):
            other = jnp.broadcast_to(into[k, c, :, :, x : x + 1], shape)
            taken = jnp.where(from_row[x], other, taken)
        return taken

    sent, stores = [], []
    count = {"face": 0, "time": 0}

    def send(kind, out, into, s_sem, r_sem, k, where):
        copy = pltpu.make_async_remote_copy(
            src_ref=out.at[k], dst_ref=into.at[k], send_sem=s_sem.at[k], recv_sem=r_sem.at[k],
            device_id=where, device_id_type=MESH,
        )
        copy.start()
        sent.append(copy)
        return copy, into, k

    def send_face(where):
        k = count["face"]
        count["face"] += 1
        return send("face", face_out, face_in, face_s, face_r, k, where)

    def send_time(where):
        k = count["time"]
        count["time"] += 1
        return send("time", time_out, time_in, time_s, time_r, k, where)

    def start_ahead(mu, half):
        for c in range(2):
            if mu == 0:
                h0[c, :, :, 0:rows] = half[c]
                face_out[count["face"], c] = half[c][:, :, 0:n2]
            elif mu == 1:
                time_out[count["time"], c] = half[c]
            elif mu == 2:
                h2[c, :, :, 0:rows] = half[c]
                for x in range(x1):
                    face_out[count["face"], c, :, :, x : x + 1] = half[c][:, :, x * n2 : x * n2 + 1]
        if mu == 0:
            return send_face(down)
        if mu == 1:
            return send_time(earlier)
        return send_face(mirror)

    def start_behind(mu, half):
        for c in range(2):
            if mu == 0:
                q0[c, :, :, 8 : 8 + rows] = half[c]
                face_out[count["face"], c] = half[c][:, :, rows - n2 : rows]
            elif mu == 1:
                time_out[count["time"], c] = half[c]
            elif mu == 2:
                q2[c, :, :, 8 : 8 + rows] = half[c]
                for x in range(x1):
                    last = x * n2 + n2 - 1
                    face_out[count["face"], c, :, :, x : x + 1] = half[c][:, :, last : last + 1]
        if mu == 0:
            return send_face(up)
        if mu == 1:
            return send_time(later)
        return send_face(mirror)

    def lane_roll(half, shift):
        return tuple(
            pltpu.roll(part.reshape(-1, lanes), shift, 1).reshape(part.shape) for part in half
        )

    def finish_ahead(mu, started, half=None):
        if mu == 3:
            return lane_roll(half, lanes - 1)
        copy, into, k = started
        copy.wait_recv()
        if mu == 0:
            h0[:, :, :, rows : rows + n2] = into[k]
            return tuple(h0[c, :, :, n2 : n2 + rows] for c in range(2))
        if mu == 1:
            return tuple(into[k, c] * sign_ahead for c in range(2))
        return tuple(
            jnp.where(at_last, from_mirror(into, k, c), h2[c, :, :, 1 : 1 + rows])
            for c in range(2)
        )

    def finish_behind(mu, started, half=None):
        if mu == 3:
            return lane_roll(half, 1)
        copy, into, k = started
        copy.wait_recv()
        if mu == 0:
            q0[:, :, :, 8 - n2 : 8] = into[k]
            return tuple(q0[c, :, :, 8 - n2 : 8 - n2 + rows] for c in range(2))
        if mu == 1:
            return tuple(into[k, c] * sign_behind for c in range(2))
        return tuple(
            jnp.where(at_first, from_mirror(into, k, c), q2[c, :, :, 7 : 7 + rows])
            for c in range(2)
        )

    def add_hop(mu, half, sign, first=False):
        order, g_re, g_im = gamma_table[mu]
        for c in range(2):
            acc[c, 0:2] = half[c] if first else acc[c, 0:2] + half[c]
        for s in range(2, 4):
            low = times_i(half[0][order[s]], half[1][order[s]], sign * g_re[s], sign * g_im[s])
            for c in range(2):
                acc[c, s] = low[c] if first else acc[c, s] + low[c]

    def finish_spinor(source, out):
        out[...] = source[...] - hopping * acc[...]

    h2[:, :, :, rows : rows + 8] = jnp.zeros_like(h2[:, :, :, rows : rows + 8])
    q2[:, :, :, 0:8] = jnp.zeros_like(q2[:, :, :, 0:8])

    def local_hop(links, source, mu, half, keep, first):
        uh = mat_vec(links, mu, half)
        if keep:
            for c in range(2):
                moved[mu, c] = uh[c]
        add_hop(mu, uh, 1, first)

    def dirac(source, out, links, keep):
        started_h, started_q = {}, {}
        for mu in (2, 1, 0):
            started_h[mu] = start_ahead(mu, project(source, mu, 1))
            started_q[mu] = start_behind(mu, dag_vec(links, mu, project(source, mu, -1)))
        for mu in (3, 0, 1, 2):
            half = finish_ahead(mu, started_h.get(mu), project(source, mu, 1) if mu == 3 else None)
            if keep:
                for c in range(2):
                    ahead[mu, c] = half[c]
            local_hop(links, source, mu, half, keep, mu == 3)
            qh = dag_vec(links, mu, project(source, mu, -1)) if mu == 3 else None
            add_hop(mu, finish_behind(mu, started_q.get(mu), qh), -1)
        finish_spinor(source, out)

    early = 6

    def force(mu, k, links, x_half):
        ux = mat_vec(links, mu, x_half)
        one = outer(ux, project(phi, mu, -1))
        two = outer(tuple(moved[mu, c] for c in range(2)), project(resp, mu, 1))
        g_re, g_im = one[0] + two[0], one[1] + two[1]
        scale = -2.0 * hopping
        third = (g_im[0, 0] + g_im[1, 1] + g_im[2, 2]) * (1.0 / 3.0)
        force_out[k, 0] = scale * (g_im[0, 0] - third)
        force_out[k, 1] = scale * (g_im[1, 1] - third)
        for n, (i, j) in enumerate(((0, 1), (0, 2), (1, 2))):
            force_out[k, 2 + 2 * n] = (0.5 * scale) * (g_im[i, j] + g_im[j, i])
            force_out[k, 3 + 2 * n] = (0.5 * scale) * (g_re[j, i] - g_re[i, j])

    def send_force(k, piece):
        rows_of = (pl.ds(0, early), pl.ds(early, 8 - early), pl.ds(0, 8))[piece]
        copy = pltpu.make_async_remote_copy(
            src_ref=force_out.at[k, rows_of], dst_ref=force_in.at[k, rows_of],
            send_sem=force_s.at[k, piece], recv_sem=force_r.at[k, piece],
            device_id=mirror, device_id_type=MESH,
        )
        copy.start()
        sent.append(copy)
        return copy

    def update(mu, k, started, links, last):
        for copy in started:
            copy.wait_recv()
        f_perm[:, 0:rows] = force_in[k]
        f_perm[:, rows : 2 * rows] = force_in[k]
        mirrored = f_perm[:, 0:rows]
        for d in range(1, x1):
            mirrored = jnp.where(turn[d], f_perm[:, d * n2 : d * n2 + rows], mirrored)
        p = []
        for n in range(8):
            real = n < 2 or n % 2 == 0
            here, there = force_out[k, n], mirrored[n]
            p.append(mom[mu, n] + step_size * (here - there if real else here + there))
        if last:
            zero = jnp.zeros((rows, lanes), F32)
            for n in range(3):
                m_out[mu, 0, n, n] = p[n] if n < 2 else -(p[0] + p[1])
                m_out[mu, 1, n, n] = zero
            for n, (i, j) in enumerate(((0, 1), (0, 2), (1, 2))):
                m_out[mu, 0, i, j] = p[2 + 2 * n]
                m_out[mu, 0, j, i] = p[2 + 2 * n]
                m_out[mu, 1, i, j] = p[3 + 2 * n]
                m_out[mu, 1, j, i] = -p[3 + 2 * n]
        else:
            for n in range(8):
                mom[mu, n] = p[n]
        e = link_exponential(p)
        u = [[(links[mu, 0, i, j], links[mu, 1, i, j]) for j in range(3)] for i in range(3)]
        for i in range(3):
            for j in range(3):
                parts = [complex_times(e[i][k2], u[k2][j]) for k2 in range(3)]
                for c in range(2):
                    u_out[mu, c, i, j] = parts[0][c] + parts[1][c] + parts[2][c]

    dirac(noise, phi, u_in, False)
    dirac(phi, resp, u_in, True)
    loads[1].wait()
    for mu in range(4):
        mom[mu, 0] = m_in[mu, 0, 0, 0]
        mom[mu, 1] = m_in[mu, 0, 1, 1]
        for n, (i, j) in enumerate(((0, 1), (0, 2), (1, 2))):
            mom[mu, 2 + 2 * n] = m_in[mu, 0, i, j]
            mom[mu, 3 + 2 * n] = m_in[mu, 1, i, j]
    for step in range(MD_STEPS):
        links = u_in if step == 0 else u_out
        last = step == MD_STEPS - 1
        started = {mu: start_ahead(mu, project(resp, mu, -1)) for mu in (2, 1, 0)}
        forces = {}
        for mu in (3, 0, 1, 2):
            x_half = finish_ahead(
                mu, started.get(mu), project(resp, mu, -1) if mu == 3 else None
            )
            force(mu, 4 * step + mu, links, x_half)
            forces[mu] = [send_force(4 * step + mu, 0 if mu == 3 else 2)]
        forces[3].append(send_force(4 * step + 3, 1))
        behind = {}
        for mu in (0, 1, 2, 3):
            update(mu, 4 * step + mu, forces[mu], links, last)
            if last:
                for n, (value, final) in enumerate(((u_out, u_final), (m_out, m_final))):
                    copy = pltpu.make_async_copy(value.at[mu], final.at[mu], store_s.at[mu, n])
                    copy.start()
                    stores.append(copy)
                continue
            qh = dag_vec(u_out, mu, project(phi, mu, -1))
            if mu != 3:
                behind[mu] = start_behind(mu, qh)
            else:
                add_hop(mu, finish_behind(mu, None, qh), -1)
            half = tuple(ahead[mu, c] for c in range(2))
            local_hop(u_out, phi, mu, half, True, mu == 0)
        if not last:
            for mu in (0, 1, 2):
                add_hop(mu, finish_behind(mu, behind[mu]), -1)
            finish_spinor(phi, resp)
    for copy in sent:
        copy.wait_send()
    for copy in stores:
        copy.wait()


def hand_over(links, momenta, links_out, momenta_out, sems):
    copies = [
        pltpu.make_async_copy(source.at[mu], out.at[mu], sems.at[n, mu])
        for mu in range(4)
        for n, (source, out) in enumerate(((links, links_out), (momenta, momenta_out)))
    ]
    for copy in copies:
        copy.start()
    for copy in copies:
        copy.wait()


def per_device(gauge_links, momenta, noise_table, noise_index, partner):
    lead = gauge_links.shape[:4]
    x1, n2, n3 = gauge_links.shape[4], gauge_links.shape[6], gauge_links.shape[7]
    rows = x1 * n2
    n_xd, n_ta = lax.axis_size("xd"), lax.axis_size("ta")
    hbm = pl.BlockSpec(memory_space=pltpu.HBM)
    half = (2, 2, 3)
    faces = 8 + 2 * MD_STEPS + 2 * (MD_STEPS - 1)
    times = 4 + MD_STEPS + (MD_STEPS - 1)
    field = (2, 4, 3, rows, n3)
    full = jax.ShapeDtypeStruct(lead + (rows, n3), F32)
    dma = pltpu.SemaphoreType.DMA
    new_links, new_momenta = pl.pallas_call(
        functools.partial(kernel, n_xd, n_ta),
        out_shape=(full, full),
        in_specs=[hbm, hbm, hbm, hbm, pl.BlockSpec(memory_space=pltpu.SMEM)],
        out_specs=(hbm, hbm),
        scratch_shapes=[
            pltpu.VMEM(lead + (rows, n3), F32),
            pltpu.VMEM(lead + (rows, n3), F32),
            pltpu.VMEM(noise_table.shape[:1] + (3, 4) + noise_table.shape[3:], F32),
            pltpu.VMEM((rows, n3), jnp.int32),
            pltpu.VMEM(lead + (rows, n3), F32),
            pltpu.VMEM(lead + (rows, n3), F32),
            pltpu.VMEM(field, F32),
            pltpu.VMEM(half + (rows + 8, n3), F32),
            pltpu.VMEM(half + (rows + 8, n3), F32),
            pltpu.VMEM(half + (rows + 8, n3), F32),
            pltpu.VMEM(half + (rows + 8, n3), F32),
            pltpu.VMEM(field, F32),
            pltpu.VMEM(field, F32),
            pltpu.VMEM(field, F32),
            pltpu.VMEM((4,) + half + (rows, n3), F32),
            pltpu.VMEM((4,) + half + (rows, n3), F32),
            pltpu.VMEM((8, 2 * rows, n3), F32),
            pltpu.VMEM((4, 8, rows, n3), F32),
            pltpu.VMEM((faces,) + half + (n2, n3), F32),
            pltpu.VMEM((faces,) + half + (n2, n3), F32),
            pltpu.VMEM((times,) + half + (rows, n3), F32),
            pltpu.VMEM((times,) + half + (rows, n3), F32),
            pltpu.VMEM((4 * MD_STEPS, 8, rows, n3), F32),
            pltpu.VMEM((4 * MD_STEPS, 8, rows, n3), F32),
            dma((faces,)), dma((faces,)), dma((times,)), dma((times,)),
            dma((4 * MD_STEPS, 3)), dma((4 * MD_STEPS, 3)),
            dma((4,)), dma((4, 2)),
        ],
        compiler_params=pltpu.CompilerParams(
            collective_id=0, has_side_effects=True, vmem_limit_bytes=60 * 1024 * 1024
        ),
    )(
        gauge_links.reshape(lead + (rows, n3)), momenta.reshape(lead + (rows, n3)),
        jnp.swapaxes(noise_table, 1, 2), noise_index.reshape(rows, n3), partner,
    )
    new_links, new_momenta = pl.pallas_call(
        hand_over,
        out_shape=(full, full),
        in_specs=[hbm, hbm],
        out_specs=(hbm, hbm),
        scratch_shapes=[dma((2, 4))],
    )(new_links, new_momenta)
    return new_links.reshape(gauge_links.shape), new_momenta.reshape(momenta.shape)


def solution(mesh):
    placed = (
        P(None, None, None, None, "xd", "ta", None, None),
        P(None, None, None, None, "xd", "ta", None, None),
        P(),
        P("xd", "ta", None, None),
        P("xd"),
    )
    return jax.shard_map(
        per_device,
        mesh=mesh,
        in_specs=placed,
        out_specs=(
            P(None, None, None, None, "xd", "ta", None, None),
            P(None, None, None, None, "xd", "ta", None, None),
        ),
        check_vma=False,
    )
```

```python
import functools

import jax
import jax.numpy as jnp
from jax import lax
from jax.experimental import pallas as pl
from jax.experimental.pallas import tpu as pltpu
from jax.sharding import PartitionSpec as P

MESH = pl.DeviceIdType.MESH
F32 = jnp.float32

MD_STEPS = 2

hopping = 0.13
step_size = 0.25
gamma_table = (
    ((3, 2, 1, 0), (0, 0, 0, 0), (1, 1, -1, -1)),
    ((2, 3, 0, 1), (1, 1, 1, 1), (0, 0, 0, 0)),
    ((3, 2, 1, 0), (-1, 1, 1, -1), (0, 0, 0, 0)),
    ((2, 3, 0, 1), (0, 0, 0, 0), (1, -1, -1, 1)),
)


def gather_noise(table, index, out, entry, split, gathered):
    rows, lanes = index.shape
    chunks = table.shape[-1] // lanes
    for c in range(chunks):
        for part in range(2):
            for colour in range(3):
                at = c * 24 + part * 12 + colour * 4
                entry[at : at + 4] = table[part, colour, :, c * lanes : (c + 1) * lanes]
    rest = entry[...]
    for n in range(3):
        piece = rest.astype(jnp.bfloat16)
        split[:, n * lanes : (n + 1) * lanes] = piece
        rest = rest - piece.astype(F32)
    lane = lax.broadcasted_iota(jnp.int32, (lanes, lanes), 0)
    for r in range(0, rows, 2):
        hot = []
        for j in range(2):
            wanted = jnp.bitwise_and(index[r + j : r + j + 1], lanes - 1)
            hot.append(jnp.where(lane == wanted, 1.0, 0.0).astype(jnp.bfloat16))
        pair = jnp.concatenate(hot, axis=1)
        picked = jnp.dot(
            split[...], jnp.concatenate([pair] * 3, axis=0), preferred_element_type=F32
        )
        for j in range(2):
            chunk = jnp.broadcast_to(lax.div(index[r + j : r + j + 1], lanes), (24, lanes))
            total = picked[0:24, j * lanes : (j + 1) * lanes]
            for c in range(1, chunks):
                value = picked[c * 24 : (c + 1) * 24, j * lanes : (j + 1) * lanes]
                total = jnp.where(chunk == c, value, total)
            gathered[:, r + j] = total
    for part in range(2):
        for colour in range(3):
            for spin in range(4):
                out[part, spin, colour] = gathered[part * 12 + colour * 4 + spin]


def times_i(re, im, g_re, g_im):
    if g_re == 1:
        return re, im
    if g_re == -1:
        return -re, -im
    if g_im == 1:
        return -im, re
    return im, -re


def project(spinor, mu, sign):
    order, g_re, g_im = gamma_table[mu]
    out_re, out_im = [], []
    for s in range(2):
        add_re, add_im = times_i(
            spinor[0, order[s]], spinor[1, order[s]], sign * g_re[s], sign * g_im[s]
        )
        out_re.append(spinor[0, s] + add_re)
        out_im.append(spinor[1, s] + add_im)
    return jnp.stack(out_re), jnp.stack(out_im)


def mat_vec(links, mu, half):
    re, im = half
    out_re = out_im = None
    for b in range(3):
        m_re, m_im = links[mu, 0, :, b][None], links[mu, 1, :, b][None]
        v_re, v_im = re[:, b : b + 1], im[:, b : b + 1]
        t_re = m_re * v_re - m_im * v_im
        t_im = m_re * v_im + m_im * v_re
        out_re = t_re if b == 0 else out_re + t_re
        out_im = t_im if b == 0 else out_im + t_im
    return out_re, out_im


def dag_vec(links, mu, half):
    re, im = half
    out_re = out_im = None
    for b in range(3):
        m_re, m_im = links[mu, 0, b][None], links[mu, 1, b][None]
        v_re, v_im = re[:, b : b + 1], im[:, b : b + 1]
        t_re = m_re * v_re + m_im * v_im
        t_im = m_re * v_im - m_im * v_re
        out_re = t_re if b == 0 else out_re + t_re
        out_im = t_im if b == 0 else out_im + t_im
    return out_re, out_im


def outer(first, second):
    out_re = out_im = None
    for s in range(2):
        f_re, f_im = first[0][s][:, None], first[1][s][:, None]
        g_re, g_im = second[0][s][None], second[1][s][None]
        t_re = f_re * g_re + f_im * g_im
        t_im = f_im * g_re - f_re * g_im
        out_re = t_re if s == 0 else out_re + t_re
        out_im = t_im if s == 0 else out_im + t_im
    return out_re, out_im


def complex_times(a, b):
    return a[0] * b[0] - a[1] * b[1], a[0] * b[1] + a[1] * b[0]


def complex_by_conj(a, b):
    return a[0] * b[0] + a[1] * b[1], a[1] * b[0] - a[0] * b[1]


def square(c):
    return c[0] * c[0] + c[1] * c[1]


def link_exponential(p):
    b = [step_size * part for part in p]
    d0, d1 = b[0], b[1]
    d2 = -(d0 + d1)
    o01, o02, o12 = (b[2], b[3]), (b[4], b[5]), (b[6], b[7])
    n01, n02, n12 = square(o01), square(o02), square(o12)
    s0 = d0 * d0 + n01 + n02
    s1 = d1 * d1 + n01 + n12
    s2 = d2 * d2 + n02 + n12
    r01 = complex_by_conj(o02, o12)
    r02 = complex_times(o01, o12)
    r12 = complex_times((o01[0], -o01[1]), o02)
    s01 = (r01[0] - d2 * o01[0], r01[1] - d2 * o01[1])
    s02 = (r02[0] - d1 * o02[0], r02[1] - d1 * o02[1])
    s12 = (r12[0] - d0 * o12[0], r12[1] - d0 * o12[1])
    c1 = 0.5 * (s0 + s1 + s2)
    c0 = (
        d0 * (d1 * d2 - n12) - d1 * n02 - d2 * n01
        + 2.0 * (r02[0] * o02[0] + r02[1] * o02[1])
    )
    q0 = (1.0 - c0 * c0 * (1.0 / 720.0), c0 * (c1 * (1.0 / 120.0) - 1.0 / 6.0))
    q1 = (c0 * (1.0 / 24.0 - c1 * (1.0 / 360.0)), 1.0 + c1 * (c1 * (1.0 / 120.0) - 1.0 / 6.0))
    q2 = (c1 * (1.0 / 24.0 - c1 * (1.0 / 720.0)) - 0.5, c0 * (1.0 / 120.0))
    e = [[None] * 3 for _ in range(3)]
    for k, (d, s) in enumerate(((d0, s0), (d1, s1), (d2, s2))):
        e[k][k] = (q0[0] + q1[0] * d + q2[0] * s, q0[1] + q1[1] * d + q2[1] * s)
    for i, j, o, s in ((0, 1, o01, s01), (0, 2, o02, s02), (1, 2, o12, s12)):
        a_re = q1[0] * o[0] + q2[0] * s[0]
        a_im = q1[0] * o[1] + q2[0] * s[1]
        b_re = q1[1] * o[0] + q2[1] * s[0]
        b_im = q1[1] * o[1] + q2[1] * s[1]
        e[i][j] = (a_re - b_im, a_im + b_re)
        e[j][i] = (a_re + b_im, b_re - a_im)
    return e


def kernel(
    n_xd, n_ta, u_hbm, m_hbm, table_hbm, index_hbm, partner, u_final, m_final,
    u_in, m_in, table, index, u_out, m_out, noise, entry, split, gathered,
    h0, q0, h2, q2, phi, resp, acc, ahead, moved, f_perm, mom,
    face_out, face_in, time_out, time_in, force_out, force_in,
    face_s, face_r, time_s, time_r, force_s, force_r, load_s, store_s,
):
    n2 = face_in.shape[-2]
    rows, lanes = phi.shape[-2:]
    x1 = rows // n2
    xd, ta = lax.axis_index("xd"), lax.axis_index("ta")
    up = {"xd": lax.rem(xd + 1, n_xd)}
    down = {"xd": lax.rem(xd + n_xd - 1, n_xd)}
    mirror = {"xd": lax.rem(xd + n_xd // 2, n_xd)}
    later = {"ta": lax.rem(ta + 1, n_ta)}
    earlier = {"ta": lax.rem(ta + n_ta - 1, n_ta)}
    sign_ahead = jnp.where(ta == n_ta - 1, -1.0, 1.0).astype(F32)
    sign_behind = jnp.where(ta == 0, -1.0, 1.0).astype(F32)

    loads = [
        pltpu.make_async_copy(u_hbm, u_in, load_s.at[0]),
        pltpu.make_async_copy(m_hbm, m_in, load_s.at[1]),
        pltpu.make_async_copy(table_hbm, table, load_s.at[2]),
        pltpu.make_async_copy(index_hbm, index, load_s.at[3]),
    ]
    for n in (3, 2, 0, 1):
        loads[n].start()
    barrier = pltpu.get_barrier_semaphore()
    for other in (up, down, mirror, later, earlier):
        pl.semaphore_signal(barrier, inc=1, device_id=other, device_id_type=MESH)
    loads[3].wait()
    loads[2].wait()
    gather_noise(table, index, noise, entry, split, gathered)
    pl.semaphore_wait(barrier, 5)
    loads[0].wait()

    row = lax.broadcasted_iota(jnp.int32, (rows, lanes), 0)
    x_row = lax.div(row, n2)
    at_first = lax.rem(row, n2) == 0
    at_last = lax.rem(row, n2) == n2 - 1
    source_row = jnp.zeros((rows, lanes), jnp.int32)
    for x in range(x1):
        source_row = jnp.where(x_row == x, lax.rem(partner[x], x1), source_row)
    from_row = [source_row == x for x in range(x1)]
    turn = [source_row == lax.rem(x_row + d, x1) for d in range(x1)]

    def from_mirror(into, k, c):
        shape = into.shape[2:4] + (rows, lanes)
        taken = jnp.broadcast_to(into[k, c, :, :, 0:1], shape)
        for x in range(1, x1):
            other = jnp.broadcast_to(into[k, c, :, :, x : x + 1], shape)
            taken = jnp.where(from_row[x], other, taken)
        return taken

    sent, stores = [], []
    count = {"face": 0, "time": 0}

    def send(kind, out, into, s_sem, r_sem, k, where):
        copy = pltpu.make_async_remote_copy(
            src_ref=out.at[k], dst_ref=into.at[k], send_sem=s_sem.at[k], recv_sem=r_sem.at[k],
            device_id=where, device_id_type=MESH,
        )
        copy.start()
        sent.append(copy)
        return copy, into, k

    def send_face(where):
        k = count["face"]
        count["face"] += 1
        return send("face", face_out, face_in, face_s, face_r, k, where)

    def send_time(where):
        k = count["time"]
        count["time"] += 1
        return send("time", time_out, time_in, time_s, time_r, k, where)

    def start_ahead(mu, half):
        for c in range(2):
            if mu == 0:
                h0[c, :, :, 0:rows] = half[c]
                face_out[count["face"], c] = half[c][:, :, 0:n2]
            elif mu == 1:
                time_out[count["time"], c] = half[c]
            elif mu == 2:
                h2[c, :, :, 0:rows] = half[c]
                for x in range(x1):
                    face_out[count["face"], c, :, :, x : x + 1] = half[c][:, :, x * n2 : x * n2 + 1]
        if mu == 0:
            return send_face(down)
        if mu == 1:
            return send_time(earlier)
        return send_face(mirror)

    def start_behind(mu, half):
        for c in range(2):
            if mu == 0:
                q0[c, :, :, 8 : 8 + rows] = half[c]
                face_out[count["face"], c] = half[c][:, :, rows - n2 : rows]
            elif mu == 1:
                time_out[count["time"], c] = half[c]
            elif mu == 2:
                q2[c, :, :, 8 : 8 + rows] = half[c]
                for x in range(x1):
                    last = x * n2 + n2 - 1
                    face_out[count["face"], c, :, :, x : x + 1] = half[c][:, :, last : last + 1]
        if mu == 0:
            return send_face(up)
        if mu == 1:
            return send_time(later)
        return send_face(mirror)

    def lane_roll(half, shift):
        return tuple(
            pltpu.roll(part.reshape(-1, lanes), shift, 1).reshape(part.shape) for part in half
        )

    def finish_ahead(mu, started, half=None):
        if mu == 3:
            return lane_roll(half, lanes - 1)
        copy, into, k = started
        copy.wait_recv()
        if mu == 0:
            h0[:, :, :, rows : rows + n2] = into[k]
            return tuple(h0[c, :, :, n2 : n2 + rows] for c in range(2))
        if mu == 1:
            return tuple(into[k, c] * sign_ahead for c in range(2))
        return tuple(
            jnp.where(at_last, from_mirror(into, k, c), h2[c, :, :, 1 : 1 + rows])
            for c in range(2)
        )

    def finish_behind(mu, started, half=None):
        if mu == 3:
            return lane_roll(half, 1)
        copy, into, k = started
        copy.wait_recv()
        if mu == 0:
            q0[:, :, :, 8 - n2 : 8] = into[k]
            return tuple(q0[c, :, :, 8 - n2 : 8 - n2 + rows] for c in range(2))
        if mu == 1:
            return tuple(into[k, c] * sign_behind for c in range(2))
        return tuple(
            jnp.where(at_first, from_mirror(into, k, c), q2[c, :, :, 7 : 7 + rows])
            for c in range(2)
        )

    def add_hop(mu, half, sign, first=False):
        order, g_re, g_im = gamma_table[mu]
        for c in range(2):
            acc[c, 0:2] = half[c] if first else acc[c, 0:2] + half[c]
        for s in range(2, 4):
            low = times_i(half[0][order[s]], half[1][order[s]], sign * g_re[s], sign * g_im[s])
            for c in range(2):
                acc[c, s] = low[c] if first else acc[c, s] + low[c]

    def finish_spinor(source, out):
        out[...] = source[...] - hopping * acc[...]

    h2[:, :, :, rows : rows + 8] = jnp.zeros_like(h2[:, :, :, rows : rows + 8])
    q2[:, :, :, 0:8] = jnp.zeros_like(q2[:, :, :, 0:8])

    def local_hop(links, source, mu, half, keep, first):
        uh = mat_vec(links, mu, half)
        if keep:
            for c in range(2):
                moved[mu, c] = uh[c]
        add_hop(mu, uh, 1, first)

    def dirac(source, out, links, keep):
        started_h, started_q = {}, {}
        for mu in (2, 1, 0):
            started_h[mu] = start_ahead(mu, project(source, mu, 1))
            started_q[mu] = start_behind(mu, dag_vec(links, mu, project(source, mu, -1)))
        for mu in (3, 0, 1, 2):
            half = finish_ahead(mu, started_h.get(mu), project(source, mu, 1) if mu == 3 else None)
            if keep:
                for c in range(2):
                    ahead[mu, c] = half[c]
            local_hop(links, source, mu, half, keep, mu == 3)
            qh = dag_vec(links, mu, project(source, mu, -1)) if mu == 3 else None
            add_hop(mu, finish_behind(mu, started_q.get(mu), qh), -1)
        finish_spinor(source, out)

    early = 6

    def force(mu, k, links, x_half):
        ux = mat_vec(links, mu, x_half)
        one = outer(ux, project(phi, mu, -1))
        two = outer(tuple(moved[mu, c] for c in range(2)), project(resp, mu, 1))
        g_re, g_im = one[0] + two[0], one[1] + two[1]
        scale = -2.0 * hopping
        third = (g_im[0, 0] + g_im[1, 1] + g_im[2, 2]) * (1.0 / 3.0)
        force_out[k, 0] = scale * (g_im[0, 0] - third)
        force_out[k, 1] = scale * (g_im[1, 1] - third)
        for n, (i, j) in enumerate(((0, 1), (0, 2), (1, 2))):
            force_out[k, 2 + 2 * n] = (0.5 * scale) * (g_im[i, j] + g_im[j, i])
            force_out[k, 3 + 2 * n] = (0.5 * scale) * (g_re[j, i] - g_re[i, j])

    def send_force(k, piece):
        rows_of = (pl.ds(0, early), pl.ds(early, 8 - early), pl.ds(0, 8))[piece]
        copy = pltpu.make_async_remote_copy(
            src_ref=force_out.at[k, rows_of], dst_ref=force_in.at[k, rows_of],
            send_sem=force_s.at[k, piece], recv_sem=force_r.at[k, piece],
            device_id=mirror, device_id_type=MESH,
        )
        copy.start()
        sent.append(copy)
        return copy

    def update(mu, k, started, links, last):
        for copy in started:
            copy.wait_recv()
        f_perm[:, 0:rows] = force_in[k]
        f_perm[:, rows : 2 * rows] = force_in[k]
        mirrored = f_perm[:, 0:rows]
        for d in range(1, x1):
            mirrored = jnp.where(turn[d], f_perm[:, d * n2 : d * n2 + rows], mirrored)
        p = []
        for n in range(8):
            real = n < 2 or n % 2 == 0
            here, there = force_out[k, n], mirrored[n]
            p.append(mom[mu, n] + step_size * (here - there if real else here + there))
        if last:
            zero = jnp.zeros((rows, lanes), F32)
            for n in range(3):
                m_out[mu, 0, n, n] = p[n] if n < 2 else -(p[0] + p[1])
                m_out[mu, 1, n, n] = zero
            for n, (i, j) in enumerate(((0, 1), (0, 2), (1, 2))):
                m_out[mu, 0, i, j] = p[2 + 2 * n]
                m_out[mu, 0, j, i] = p[2 + 2 * n]
                m_out[mu, 1, i, j] = p[3 + 2 * n]
                m_out[mu, 1, j, i] = -p[3 + 2 * n]
        else:
            for n in range(8):
                mom[mu, n] = p[n]
        e = link_exponential(p)
        u = [[(links[mu, 0, i, j], links[mu, 1, i, j]) for j in range(3)] for i in range(3)]
        for i in range(3):
            for j in range(3):
                parts = [complex_times(e[i][k2], u[k2][j]) for k2 in range(3)]
                for c in range(2):
                    u_out[mu, c, i, j] = parts[0][c] + parts[1][c] + parts[2][c]

    dirac(noise, phi, u_in, False)
    dirac(phi, resp, u_in, True)
    loads[1].wait()
    for mu in range(4):
        mom[mu, 0] = m_in[mu, 0, 0, 0]
        mom[mu, 1] = m_in[mu, 0, 1, 1]
        for n, (i, j) in enumerate(((0, 1), (0, 2), (1, 2))):
            mom[mu, 2 + 2 * n] = m_in[mu, 0, i, j]
            mom[mu, 3 + 2 * n] = m_in[mu, 1, i, j]
    for step in range(MD_STEPS):
        links = u_in if step == 0 else u_out
        last = step == MD_STEPS - 1
        started = {mu: start_ahead(mu, project(resp, mu, -1)) for mu in (2, 1, 0)}
        forces = {}
        for mu in (3, 0, 1, 2):
            x_half = finish_ahead(
                mu, started.get(mu), project(resp, mu, -1) if mu == 3 else None
            )
            force(mu, 4 * step + mu, links, x_half)
            forces[mu] = [send_force(4 * step + mu, 0 if mu == 3 else 2)]
        forces[3].append(send_force(4 * step + 3, 1))
        behind = {}
        for mu in (0, 1, 2, 3):
            update(mu, 4 * step + mu, forces[mu], links, last)
            if last:
                for n, (value, final) in enumerate(((u_out, u_final), (m_out, m_final))):
                    copy = pltpu.make_async_copy(value.at[mu], final.at[mu], store_s.at[mu, n])
                    copy.start()
                    stores.append(copy)
                continue
            qh = dag_vec(u_out, mu, project(phi, mu, -1))
            if mu != 3:
                behind[mu] = start_behind(mu, qh)
            else:
                add_hop(mu, finish_behind(mu, None, qh), -1)
            half = tuple(ahead[mu, c] for c in range(2))
            local_hop(u_out, phi, mu, half, True, mu == 0)
        if not last:
            for mu in (0, 1, 2):
                add_hop(mu, finish_behind(mu, behind[mu]), -1)
            finish_spinor(phi, resp)
    for copy in sent:
        copy.wait_send()
    for copy in stores:
        copy.wait()


def hand_over(links, momenta, links_out, momenta_out, stage, in_s, out_s):
    pairs = ((links, links_out), (momenta, momenta_out))
    taken, given = [], []
    for n, (source, out) in enumerate(pairs):
        for mu in range(4):
            slot = stage.at[n, mu]
            taken.append(pltpu.make_async_copy(source.at[mu], slot, in_s.at[n, mu]))
            given.append(pltpu.make_async_copy(slot, out.at[mu], out_s.at[n, mu]))
    for copy in taken:
        copy.start()
    for arrived, leaving in zip(taken, given):
        arrived.wait()
        leaving.start()
    for copy in given:
        copy.wait()


def per_device(gauge_links, momenta, noise_table, noise_index, partner):
    lead = gauge_links.shape[:4]
    x1, n2, n3 = gauge_links.shape[4], gauge_links.shape[6], gauge_links.shape[7]
    rows = x1 * n2
    n_xd, n_ta = lax.axis_size("xd"), lax.axis_size("ta")
    hbm = pl.BlockSpec(memory_space=pltpu.HBM)
    half = (2, 2, 3)
    chunks = noise_table.shape[-1] // n3
    faces = 8 + 2 * MD_STEPS + 2 * (MD_STEPS - 1)
    times = 4 + MD_STEPS + (MD_STEPS - 1)
    field = (2, 4, 3, rows, n3)
    full = jax.ShapeDtypeStruct(lead + (rows, n3), F32)
    dma = pltpu.SemaphoreType.DMA
    new_links, new_momenta = pl.pallas_call(
        functools.partial(kernel, n_xd, n_ta),
        out_shape=(full, full),
        in_specs=[hbm, hbm, hbm, hbm, pl.BlockSpec(memory_space=pltpu.SMEM)],
        out_specs=(hbm, hbm),
        scratch_shapes=[
            pltpu.VMEM(lead + (rows, n3), F32),
            pltpu.VMEM(lead + (rows, n3), F32),
            pltpu.VMEM(noise_table.shape[:1] + (3, 4) + noise_table.shape[3:], F32),
            pltpu.VMEM((rows, n3), jnp.int32),
            pltpu.VMEM(lead + (rows, n3), F32),
            pltpu.VMEM(lead + (rows, n3), F32),
            pltpu.VMEM(field, F32),
            pltpu.VMEM((24 * chunks, n3), F32),
            pltpu.VMEM((24 * chunks, 3 * n3), jnp.bfloat16),
            pltpu.VMEM((24, rows, n3), F32),
            pltpu.VMEM(half + (rows + 8, n3), F32),
            pltpu.VMEM(half + (rows + 8, n3), F32),
            pltpu.VMEM(half + (rows + 8, n3), F32),
            pltpu.VMEM(half + (rows + 8, n3), F32),
            pltpu.VMEM(field, F32),
            pltpu.VMEM(field, F32),
            pltpu.VMEM(field, F32),
            pltpu.VMEM((4,) + half + (rows, n3), F32),
            pltpu.VMEM((4,) + half + (rows, n3), F32),
            pltpu.VMEM((8, 2 * rows, n3), F32),
            pltpu.VMEM((4, 8, rows, n3), F32),
            pltpu.VMEM((faces,) + half + (n2, n3), F32),
            pltpu.VMEM((faces,) + half + (n2, n3), F32),
            pltpu.VMEM((times,) + half + (rows, n3), F32),
            pltpu.VMEM((times,) + half + (rows, n3), F32),
            pltpu.VMEM((4 * MD_STEPS, 8, rows, n3), F32),
            pltpu.VMEM((4 * MD_STEPS, 8, rows, n3), F32),
            dma((faces,)), dma((faces,)), dma((times,)), dma((times,)),
            dma((4 * MD_STEPS, 3)), dma((4 * MD_STEPS, 3)),
            dma((4,)), dma((4, 2)),
        ],
        compiler_params=pltpu.CompilerParams(
            collective_id=0, has_side_effects=True, vmem_limit_bytes=60 * 1024 * 1024
        ),
    )(
        gauge_links.reshape(lead + (rows, n3)), momenta.reshape(lead + (rows, n3)),
        jnp.swapaxes(noise_table, 1, 2), noise_index.reshape(rows, n3), partner,
    )
    new_links, new_momenta = pl.pallas_call(
        hand_over,
        out_shape=(full, full),
        in_specs=[hbm, hbm],
        out_specs=(hbm, hbm),
        scratch_shapes=[pltpu.VMEM((2,) + lead + (rows, n3), F32), dma((2, 4)), dma((2, 4))],
    )(new_links, new_momenta)
    return new_links.reshape(gauge_links.shape), new_momenta.reshape(momenta.shape)


def solution(mesh):
    placed = (
        P(None, None, None, None, "xd", "ta", None, None),
        P(None, None, None, None, "xd", "ta", None, None),
        P(),
        P("xd", "ta", None, None),
        P("xd"),
    )
    return jax.shard_map(
        per_device,
        mesh=mesh,
        in_specs=placed,
        out_specs=(
            P(None, None, None, None, "xd", "ta", None, None),
            P(None, None, None, None, "xd", "ta", None, None),
        ),
        check_vma=False,
    )
```
